256 devices in a mesh: section: 16 (over z, x_hi), tensor: 16 (over x_lo, y, core).
Axes of the slice: x: 4 (x_hi: 2, x_lo: 2; x = x_hi * 2 + x_lo), y: 4, z: 8, core: 2. Of those that a mesh axis runs over, the one named last changes fastest.
Arguments:
- handed_state: bfloat16 [16, 2, 512, 4096], P('section', None, 'tensor'), may hold values from -6 to 6
- handed_grad: bfloat16 [16, 2, 512, 4096], P('section', None, 'tensor'), may hold values from -6 to 6
- top_state: bfloat16 [2, 512, 4096], P(None, 'tensor'), may hold values from -6 to 6
- loss_grad: bfloat16 [2, 512, 4096], P(None, 'tensor'), may hold values from -6 to 6
- ln_gain: bfloat16 [16, 4096], P('section'), may hold values from 0.099609375 to 1.8984375
- w_qkv: bfloat16 [16, 3, 4096, 4096], P('section', None, None, 'tensor'), may hold values from -0.09375 to 0.09375
- w_out: bfloat16 [16, 4096, 4096], P('section', 'tensor'), may hold values from -0.375 to 0.375
Outputs:
- rebuilt: bfloat16 [16, 2, 512, 4096], P('section', None, 'tensor')
- input_grad: bfloat16 [16, 2, 512, 4096], P('section', None, 'tensor')
The draws below stay inside these ranges and needn't reach their ends.
All inputs are finite; a program needn't handle non-finite values.
Results may differ from the reference program's by a relative error of at most 0.018.
Values may be sent and summed in bfloat16 or wider, within the bound.
A program may use at most 64 MiB of HBM per device.

```python
import jax
import jax.numpy as jnp
from jax import lax

D = 4096
HEADS = 32
HD = 128
TOK = 256
IMAGES = 2
TOKENS = 512
N_SECTION = 16
N_TENSOR = 16


def shard_levels(own_key, dims, split, least, high):
    def one(dim, blocks):
        steps = jax.random.uniform(jax.random.fold_in(jax.random.fold_in(own_key, 6), dim), (blocks,), jnp.float32, least / len(split), high / len(split))
        return jnp.repeat(jnp.exp(steps), dims[dim] // blocks).reshape((-1,) + (1,) * (len(dims) - dim - 1))

    gain = one(*split[0])
    for cut in split[1:]:
        gain = gain * one(*cut)
    return gain


def bell_draw(stream_key, extent, deviation, bound, split=(), dtype=jnp.bfloat16):
    factor_of = shard_levels(stream_key, extent, split, -0.22, 0.18) if split else 1.0
    entries = jax.random.normal(stream_key, extent, jnp.float32) * deviation * factor_of
    return jnp.minimum(jnp.maximum(entries, -bound), bound).astype(dtype)


def setup_inputs(seed: int = 0) -> dict:
    key_list = jax.random.split(jax.random.key(seed), 8)
    handed_state = bell_draw(key_list[0], (N_SECTION, 2, TOKENS, D), 1.0, 6.0, ((0, 16), (2, 16)))
    handed_grad = bell_draw(key_list[1], (N_SECTION, 2, TOKENS, D), 1.0, 6.0, ((0, 16), (2, 16)))
    top_state = bell_draw(key_list[2], (2, TOKENS, D), 1.0, 6.0, ((1, 16),))
    loss_grad = bell_draw(key_list[3], (2, TOKENS, D), 1.0, 6.0, ((1, 16),))
    ln_gain = jnp.clip(1.0 + 0.18 * jax.random.normal(key_list[4], (N_SECTION, D), jnp.float32), 0.099609375, 1.8984375).astype(jnp.bfloat16)
    w_qkv = bell_draw(key_list[5], (N_SECTION, 3, D, HEADS * HD), D ** -0.5, 0.09375, ((0, 16), (3, 16)))
    w_out = bell_draw(key_list[6], (N_SECTION, HEADS * HD, D), (4.0 * (HEADS * HD) ** -0.5), 0.375, ((0, 16), (1, 16)))
    return {"handed_state": handed_state, "handed_grad": handed_grad, "top_state": top_state, "loss_grad": loss_grad, "ln_gain": ln_gain, "w_qkv": w_qkv, "w_out": w_out}


def normalize(rows, norm_gain):
    values = rows.astype(jnp.float32)
    row_mean = lax.optimization_barrier(jnp.mean(values, axis=-1, keepdims=True))
    centred = values - row_mean
    inv_scale = lax.rsqrt(lax.optimization_barrier(jnp.mean(centred * centred, axis=-1, keepdims=True)) + 1e-06)
    unit_rows = centred * inv_scale
    return ((unit_rows * norm_gain.astype(jnp.float32)).astype(jnp.bfloat16), unit_rows, inv_scale)

def unit_norm(values):
    row_mean = lax.optimization_barrier(jnp.mean(values, axis=-1, keepdims=True))
    centred = values - row_mean
    inv_scale = lax.rsqrt(lax.optimization_barrier(jnp.mean(centred * centred, axis=-1, keepdims=True)) + 1e-06)
    return (centred * inv_scale, inv_scale)

def norm_back(grad_unit, unit_rows, inv_scale):
    first_mean = lax.optimization_barrier(jnp.mean(grad_unit, axis=-1, keepdims=True))
    second_mean = lax.optimization_barrier(jnp.mean(grad_unit * unit_rows, axis=-1, keepdims=True))
    return (grad_unit - first_mean - unit_rows * second_mean) * inv_scale

def round_trip(values):
    return lax.optimization_barrier(values.astype(jnp.bfloat16)).astype(jnp.float32)

def core_forward(query_raw, key_raw, value_rows):
    query_unit, query_scale = unit_norm(query_raw)
    key_unit, key_scale = unit_norm(key_raw)
    query_half = query_unit.astype(jnp.bfloat16)
    key_half = key_unit.astype(jnp.bfloat16)
    scores = jnp.einsum('iqhc,ikhc->ihqk', query_half.astype(jnp.float32), key_half.astype(jnp.float32)) * HD ** (-0.5)
    exponent = jnp.exp(scores)
    attn_prob = exponent / lax.optimization_barrier(jnp.sum(exponent, axis=-1, keepdims=True))
    prob_half = attn_prob.astype(jnp.bfloat16)
    mixed = jnp.einsum('ihqk,ikhc->iqhc', prob_half.astype(jnp.float32), value_rows.astype(jnp.float32)).astype(jnp.bfloat16)
    return (mixed, (query_unit, query_scale, key_unit, key_scale, query_half, key_half, attn_prob, prob_half))

def core_backward(mixed_grad, value_rows, saved):
    query_unit, query_scale, key_unit, key_scale, query_half, key_half, attn_prob, prob_half = saved
    prob_grad = jnp.einsum('iqhc,ikhc->ihqk', mixed_grad.astype(jnp.float32), value_rows.astype(jnp.float32))
    value_grad = jnp.einsum('ihqk,iqhc->ikhc', prob_half.astype(jnp.float32), mixed_grad.astype(jnp.float32)).astype(jnp.bfloat16)
    inner = lax.optimization_barrier(jnp.sum(prob_grad * attn_prob, axis=-1, keepdims=True))
    score_grad = (attn_prob * (prob_grad - inner) * HD ** (-0.5)).astype(jnp.bfloat16)
    query_part = jnp.einsum('ihqk,ikhc->iqhc', score_grad.astype(jnp.float32), key_half.astype(jnp.float32))
    key_part = jnp.einsum('ihqk,iqhc->ikhc', score_grad.astype(jnp.float32), query_half.astype(jnp.float32))
    query_grad = norm_back(query_part, query_unit, query_scale).astype(jnp.bfloat16)
    key_grad = norm_back(key_part, key_unit, key_scale).astype(jnp.bfloat16)
    return (query_grad, key_grad, value_grad)

def sublayer(rows, norm_gain, weights, out_weights):
    normed, unit_rows, inv_scale = normalize(rows, norm_gain)
    query_raw = jnp.dot(normed, weights[0], preferred_element_type=jnp.float32).reshape(IMAGES, TOK, HEADS, HD)
    key_raw = jnp.dot(normed, weights[1], preferred_element_type=jnp.float32).reshape(IMAGES, TOK, HEADS, HD)
    value_rows = jnp.dot(normed, weights[2], preferred_element_type=jnp.float32).astype(jnp.bfloat16).reshape(IMAGES, TOK, HEADS, HD)
    mixed, saved = core_forward(query_raw, key_raw, value_rows)
    groups = mixed.reshape(TOKENS, N_TENSOR, -1).astype(jnp.float32)
    partial_value = jnp.einsum('tgc,gcd->gtd', groups, out_weights.reshape(N_TENSOR, -1, D).astype(jnp.float32), precision=lax.Precision.HIGHEST)
    head_total = lax.optimization_barrier(jnp.sum(round_trip(partial_value), axis=0))
    return (head_total, (unit_rows, inv_scale, value_rows, saved))

def grouped(grads, matrix):
    return jnp.einsum('tgc,dgc->gtd', grads.reshape(TOKENS, N_TENSOR, -1).astype(jnp.float32), matrix.reshape(D, N_TENSOR, -1).astype(jnp.float32), precision=lax.Precision.HIGHEST)

def backward_pass(state, cotangent, norm_gain, weights, out_weights):
    first_out, second_out = (state[0], state[1])
    first_grad, second_grad = (cotangent[0], cotangent[1])
    head_total, cache = sublayer(first_out, norm_gain, weights, out_weights)
    unit_rows, inv_scale, value_rows, saved = cache
    first_in = (second_out.astype(jnp.float32) - head_total).astype(jnp.bfloat16)
    mixed_grad = jnp.dot(second_grad, out_weights.T, preferred_element_type=jnp.float32).astype(jnp.bfloat16).reshape(IMAGES, TOK, HEADS, HD)
    query_grad, key_grad, value_grad = core_backward(mixed_grad, value_rows, saved)
    partial_value = grouped(query_grad, weights[0]) + grouped(key_grad, weights[1]) + grouped(value_grad, weights[2])
    normed_grad = lax.optimization_barrier(jnp.sum(round_trip(partial_value), axis=0))
    input_part = norm_back(normed_grad * norm_gain.astype(jnp.float32), unit_rows, inv_scale)
    second_in_grad = (first_grad.astype(jnp.float32) + input_part).astype(jnp.bfloat16)
    return (jnp.stack([first_in, first_out]), jnp.stack([second_grad, second_in_grad]))

def reference(handed_state, handed_grad, top_state, loss_grad, ln_gain, w_qkv, w_out):
    rebuilt_all, grads_all = ([], [])
    for position in range(N_SECTION):
        if position == N_SECTION - 1:
            state_now, grad_now = (top_state, loss_grad)
        else:
            state_now, grad_now = (handed_state[position + 1], handed_grad[position + 1])
        rebuilt_part, grad_part = backward_pass(state_now, grad_now, ln_gain[position], w_qkv[position], w_out[position])
        rebuilt_all.append(rebuilt_part)
        grads_all.append(grad_part)
    return (jnp.stack(rebuilt_all), jnp.stack(grads_all))
```

```python
import functools

import jax
import jax.numpy as jnp
from jax import lax
from jax.experimental import pallas as pl
from jax.experimental.pallas import tpu as pltpu
from jax.sharding import PartitionSpec as P

HD = 128
MESH = pl.DeviceIdType.MESH
F32 = jnp.float32
BF16 = jnp.bfloat16
R = 32
N_COPIES = 128


def mean_last(values):
    return jnp.mean(values, axis=-1, keepdims=True)


def unit_norm(values):
    centred = values - mean_last(values)
    inv_scale = lax.rsqrt(mean_last(centred * centred) + 1e-06)
    return centred * inv_scale, inv_scale


def norm_back(grad_unit, unit_rows, inv_scale):
    first_mean = mean_last(grad_unit)
    second_mean = mean_last(grad_unit * unit_rows)
    return (grad_unit - first_mean - unit_rows * second_mean) * inv_scale


def dot(a, b, dims):
    return lax.dot_general(a, b, ((dims[:1], dims[1:]), ((), ())), preferred_element_type=F32)


class Net:
    def __init__(self, send_sem, recv_sem):
        self.send_sem, self.recv_sem, self.copies = send_sem, recv_sem, []

    def make(self, src, dst, dev):
        i = len(self.copies)
        copy = pltpu.make_async_remote_copy(
            src_ref=src, dst_ref=dst, send_sem=self.send_sem.at[i], recv_sem=self.recv_sem.at[i],
            device_id=dev, device_id_type=MESH,
        )
        self.copies.append(copy)
        return copy

    def send(self, src, dst, dev):
        copy = self.make(src, dst, dev)
        copy.start()
        return copy


def kernel(
    n_section, state_ref, grad_ref, top_ref, loss_ref, gain_ref, wqkv_ref, wout_ref,
    rebuilt_ref, grads_ref,
    g1, g2, nb, e_buf, gc0, gc1, wq, wo, p1, q1, p2, q2, rx1, rp1, rm1, rx2, rp2, rm2,
    qkv, units, scales, probs, mixed, mgrad, dgrad, gain, out0, out1,
    send_sem, recv_sem, load_sem, out_sem,
):
    D = g1.shape[-1]
    tiles = D // 128
    na = -(-tiles * 5 // 18)
    a_w, half = na * 128, D // 2
    A0, B0, B1, A1 = (0, a_w), (a_w, half), (half, D - a_w), (D - a_w, D)
    BB, C0, C1, ALL = (a_w, D - a_w), (0, half), (half, D), (0, D)
    CH = (C0, C1)

    s = lax.axis_index("section")
    t = lax.axis_index("tensor")
    x, y, c = t // 8, (t // 2) % 4, t % 2
    ox = 1 - x
    yp, ym, y2 = (y + 1) % 4, (y + 3) % 4, (y + 2) % 4

    def dev(xx, yy, cc):
        return (s, xx * 8 + yy * 2 + cc)

    d_yp, d_ym, d_x, d_c = dev(x, yp, c), dev(x, ym, c), dev(ox, y, c), dev(x, y, 1 - c)
    d_prev = ((s + n_section - 1) % n_section, ox * 8 + y * 2 + c)
    d_next = ((s + 1) % n_section, ox * 8 + y * 2 + c)

    def row(yo, cc=None):
        return pl.multiple_of(((c if cc is None else cc) * 4 + yo) * R, R)

    def T(buf, xo, yo, cols, cc=None):
        return buf.at[xo, pl.ds(row(yo, cc), R), pl.ds(cols[0], cols[1] - cols[0])]

    def slot(buf, i, cols):
        return buf.at[i, :, pl.ds(cols[0], cols[1] - cols[0])]

    barrier = pltpu.get_barrier_semaphore()
    for d in (d_yp, d_ym, d_x, d_c, d_prev, d_next):
        pl.semaphore_signal(barrier, inc=1, device_id=d, device_id_type=MESH)
    pl.semaphore_wait(barrier, 6)

    net = Net(send_sem, recv_sem)

    def shift(first_src, src, k, cols, dst):
        cut = pl.ds(cols[0], cols[1] - cols[0])
        here = net.make(src.at[0, k, :, cut], dst, d_prev)
        net.copies.pop()
        last = net.make(first_src.at[k, :, cut], dst, d_prev)

        @pl.when(s == 0)
        def _():
            last.start()

        @pl.when(s != 0)
        def _():
            here.start()

        return last

    sh_c = [shift(top_ref, state_ref, 0, k, T(g1, x, y, k)) for k in CH]

    loads = [
        pltpu.make_async_copy(gain_ref, gain, load_sem.at[0]),
        pltpu.make_async_copy(wqkv_ref.at[0], wq, load_sem.at[1]),
        pltpu.make_async_copy(wout_ref.at[0], wo, load_sem.at[2]),
    ]
    for load in loads:
        load.start()

    def first_hop(buf, arrivals):
        one = []
        for k in range(2):
            arrivals[k].wait_recv()
            one.append([net.send(T(buf, ox, y, CH[k]), T(buf, ox, y, CH[k]), d) for d in (d_yp, d_ym, d_x)])
        return one

    def fwd(buf, xo, yo, cols, d):
        return net.send(T(buf, xo, yo, cols), T(buf, xo, yo, cols), d)

    def core_send(buf, xo, yo):
        return fwd(buf, xo, yo, ALL, d_c)

    def second_hop(buf, one):
        for copy in one[0]:
            copy.wait_recv()
        two = {}
        two["up"] = fwd(buf, ox, ym, C0, d_yp)
        two["xb0m"] = fwd(buf, ox, ym, B0, d_x)
        two["xb0p"] = fwd(buf, ox, yp, B0, d_x)
        two["a0u"] = fwd(buf, x, y, A0, d_yp)
        two["a0d"] = fwd(buf, x, y, A0, d_ym)
        for copy in one[1]:
            copy.wait_recv()
        two["down"] = fwd(buf, ox, yp, C1, d_ym)
        two["xb1p"] = fwd(buf, ox, yp, B1, d_x)
        two["xb1m"] = fwd(buf, ox, ym, B1, d_x)
        two["a1d"] = fwd(buf, x, y, A1, d_ym)
        two["a1u"] = fwd(buf, x, y, A1, d_yp)
        return two

    def third_hop(buf, two):
        three = {}
        two["up"].wait_recv()
        three["xb0"] = fwd(buf, ox, y2, B0, d_x)
        two["down"].wait_recv()
        three["xb1"] = fwd(buf, ox, y2, B1, d_x)
        two["a0u"].wait_recv()
        three["a0"] = fwd(buf, x, ym, A0, d_yp)
        two["a1d"].wait_recv()
        three["a1"] = fwd(buf, x, yp, A1, d_ym)
        return three

    def normalize(xo, yo, cc):
        r0 = row(yo, cc)
        rows = g1[xo, pl.ds(r0, R), :].astype(F32)
        unit_rows, _ = unit_norm(rows)
        nb[xo, pl.ds(r0, R), :] = (unit_rows * gain[...].astype(F32)).astype(BF16)

    def wait_rest(two, three):
        for k in ("xb0m", "xb1m", "xb0p", "xb1p", "a1u", "a0d"):
            two[k].wait_recv()

    one = first_hop(g1, sh_c)
    sh_g = [shift(loss_ref, grad_ref, 1, k, T(g2, x, y, k)) for k in CH]
    cs = [core_send(g1, ox, y)]
    loads[0].wait()
    normalize(ox, y, c)
    two = second_hop(g1, one)
    sh_e = shift(top_ref, state_ref, 1, ALL, e_buf)
    sh_gc = shift(loss_ref, grad_ref, 0, ALL, gc0)
    cs += [core_send(g1, ox, ym), core_send(g1, ox, yp), core_send(g1, x, y)]
    three = third_hop(g1, two)
    cs.append(core_send(g1, ox, y2))
    one_g = first_hop(g2, sh_g)
    cs_g = [core_send(g2, ox, y)]
    own_order = [(ox, y), (ox, ym), (ox, yp), (x, y), (ox, y2), (x, ym), (x, yp), (x, y2)]
    for xo, yo in own_order[1:5]:
        normalize(xo, yo, c)
    for i in range(5):
        cs[i].wait_recv()
        normalize(*own_order[i], 1 - c)
    wait_rest(two, three)
    cs.append(core_send(g1, x, ym))
    cs.append(core_send(g1, x, yp))
    for k in ("xb0", "xb1", "a0", "a1"):
        three[k].wait_recv()
    cs.append(core_send(g1, x, y2))
    for xo, yo in own_order[5:]:
        normalize(xo, yo, c)
    two_g = second_hop(g2, one_g)
    cs_g += [core_send(g2, ox, ym), core_send(g2, ox, yp), core_send(g2, x, y)]
    for i in range(5, 8):
        cs[i].wait_recv()
        normalize(*own_order[i], 1 - c)
    keep_c = pltpu.make_async_copy(T(g1, x, y, ALL), rebuilt_ref.at[0, 1], out_sem.at[0])
    keep_c.start()

    def project(i):
        @pl.loop(0, 3)
        def _(k):
            raw = dot(nb[i], wq[k], (1, 0))
            qkv[k, i, 0] = raw[:, :HD]
            qkv[k, i, 1] = raw[:, HD:]

    def forward(i):
        for h in range(2):
            q_unit, q_scale = unit_norm(qkv[0, i, h])
            k_unit, k_scale = unit_norm(qkv[1, i, h])
            units[0, i, h] = q_unit
            units[1, i, h] = k_unit
            scales[0, i, h] = q_scale
            scales[1, i, h] = k_scale
            scores = dot(q_unit.astype(BF16), k_unit.astype(BF16), (1, 1)) * HD ** (-0.5)
            exponent = jnp.exp(scores)
            prob = exponent * (1.0 / jnp.sum(exponent, axis=-1, keepdims=True))
            probs[i, h] = prob
            value = qkv[2, i, h].astype(BF16)
            mixed[i, :, h * HD:(h + 1) * HD] = dot(prob.astype(BF16), value, (1, 0)).astype(BF16)

    step = min(512, D)

    def out_project(i):
        @pl.loop(0, D // step)
        def _(n):
            cut = pl.ds(pl.multiple_of(n * step, step), step)
            p1[i, :, cut] = dot(mixed[i], wo[:, cut], (1, 0)).astype(BF16)

    def pair_send(p, q, i):
        half_rows = p.at[i, pl.ds(pl.multiple_of((1 - c) * 4 * R, R), 4 * R), :]
        return net.send(half_rows, q.at[i], d_c)

    def pair_sum(p, q, i, copy):
        copy.wait_recv()

        @pl.loop(0, 4)
        def _(b):
            r0 = row(b)
            q_rows = q[i, pl.ds(pl.multiple_of(b * R, R), R), :].astype(F32)
            p[i, pl.ds(r0, R), :] = (p[i, pl.ds(r0, R), :].astype(F32) + q_rows).astype(BF16)

    loads[1].wait()
    project(ox)
    three_g = third_hop(g2, two_g)
    cs_g.append(core_send(g2, ox, y2))
    project(x)
    wait_rest(two_g, three_g)
    cs_g.append(core_send(g2, x, ym))
    cs_g.append(core_send(g2, x, yp))
    forward(ox)
    loads[2].wait()
    out_project(ox)
    pair1 = [pair_send(p1, q1, ox)]
    for k in ("xb0", "xb1", "a0", "a1"):
        three_g[k].wait_recv()
    cs_g.append(core_send(g2, x, y2))
    forward(x)
    out_project(x)
    pair1.append(pair_send(p1, q1, x))
    sh_gc.wait_recv()
    hop_gc = net.send(gc0, gc1, d_x)
    sh_e.wait_recv()

    def add_to(p, xo, yo, recv, i, cols):
        cut = pl.ds(cols[0], cols[1] - cols[0])
        r0 = row(yo)
        mine = p[xo, pl.ds(r0, R), cut].astype(F32)
        p[xo, pl.ds(r0, R), cut] = (mine + recv[i, :, cut].astype(F32)).astype(BF16)

    class Scatter:
        def __init__(self, p, rx, rp, rm):
            self.p, self.rx, self.rp, self.rm, self.copies = p, rx, rp, rm, {}

        def out(self, name, xo, yo, cols, recv, i, d):
            self.copies[name] = net.send(T(self.p, xo, yo, cols), slot(recv, i, cols), d)

        def take(self, name, xo, yo, recv, i, cols):
            self.copies[name].wait_recv()
            add_to(self.p, xo, yo, recv, i, cols)

        def far(self):
            rx, rp, rm = self.rx, self.rp, self.rm
            self.out("x0", ox, y2, BB, rx, 0, d_x)
            self.out("p0", ox, y2, A0, rp, 0, d_ym)
            self.out("m0", ox, y2, A1, rm, 0, d_yp)
            self.out("x1", ox, yp, BB, rx, 1, d_x)
            self.out("x2", ox, ym, BB, rx, 2, d_x)
            self.out("p2l", ox, ym, A1, rp, 2, d_ym)
            self.out("m2l", ox, yp, A0, rm, 2, d_yp)
            self.out("x3b", ox, y, BB, rx, 3, d_x)

        def near(self):
            rp, rm = self.rp, self.rm
            self.out("p1", x, y2, A0, rp, 1, d_ym)
            self.out("m1", x, y2, A1, rm, 1, d_yp)
            self.out("p3l", x, ym, A1, rp, 3, d_ym)
            self.out("m3l", x, yp, A0, rm, 3, d_yp)

        def mid_far(self):
            rp, rm = self.rp, self.rm
            self.take("p0", ox, ym, rp, 0, A0)
            self.out("p2", ox, ym, A0, rp, 2, d_ym)
            self.take("m0", ox, yp, rm, 0, A1)
            self.out("m2", ox, yp, A1, rm, 2, d_yp)

        def mid_x(self):
            rx, rp, rm = self.rx, self.rp, self.rm
            self.take("x0", x, y2, rx, 0, BB)
            self.out("p1b", x, y2, B0, rp, 1, d_ym)
            self.out("m1b", x, y2, B1, rm, 1, d_yp)

        def mid_near(self):
            rp, rm = self.rp, self.rm
            self.take("p1", x, ym, rp, 1, A0)
            self.out("p3", x, ym, A0, rp, 3, d_ym)
            self.take("m1", x, yp, rm, 1, A1)
            self.out("m3", x, yp, A1, rm, 3, d_yp)

        def mid_x2(self):
            rx, rp, rm = self.rx, self.rp, self.rm
            self.take("x1", x, yp, rx, 1, BB)
            self.out("m3bl", x, yp, B0, rm, 3, d_yp)
            self.take("x2", x, ym, rx, 2, BB)
            self.out("p3bl", x, ym, B1, rp, 3, d_ym)

        def late_y(self):
            rp, rm = self.rp, self.rm
            self.take("p1b", x, ym, rp, 1, B0)
            self.out("p3b", x, ym, B0, rp, 3, d_ym)
            self.take("m1b", x, yp, rm, 1, B1)
            self.out("m3b", x, yp, B1, rm, 3, d_yp)

        def late_x(self):
            rx, rp, rm = self.rx, self.rp, self.rm
            self.take("p2l", ox, y, rp, 2, A1)
            self.take("m2", ox, y, rm, 2, A1)
            self.out("x3a1", ox, y, A1, rx, 3, d_x)
            self.take("m2l", ox, y, rm, 2, A0)
            self.take("p2", ox, y, rp, 2, A0)
            self.out("x3a0", ox, y, A0, rx, 3, d_x)

        def end(self):
            for name in ("x3b", "p3l", "m3l", "p3", "m3", "m3bl", "p3bl", "p3b", "m3b", "x3a1", "x3a0"):
                self.copies[name].wait_recv()

        def total(self):
            p, rx, rp, rm = self.p, self.rx, self.rp, self.rm
            mine = p[x, pl.ds(row(y), R), :].astype(F32) + rx[3].astype(F32)
            return mine + (rp[3].astype(F32) + rm[3].astype(F32))

    rs1 = Scatter(p1, rx1, rp1, rm1)
    pair_sum(p1, q1, ox, pair1[0])
    r_e = row(y)
    p1[ox, pl.ds(r_e, R), :] = (p1[ox, pl.ds(r_e, R), :].astype(F32) - e_buf[...].astype(F32)).astype(BF16)
    rs1.far()
    pair_sum(p1, q1, x, pair1[1])
    rs1.near()

    for i in range(8):
        cs_g[i].wait_recv()

    def mixed_back(i):
        mgrad[i] = dot(g2[i], wo[...], (1, 1)).astype(BF16)

    def backward(i):
        for h in range(2):
            cols = slice(h * HD, (h + 1) * HD)
            mg = mgrad[i, :, cols]
            value = qkv[2, i, h].astype(BF16)
            prob = probs[i, h]
            prob_grad = dot(mg, value, (1, 1))
            dgrad[2, i, :, cols] = dot(prob.astype(BF16), mg, (0, 0)).astype(BF16)
            inner = jnp.sum(prob_grad * prob, axis=-1, keepdims=True)
            score_grad = (prob * (prob_grad - inner) * HD ** (-0.5)).astype(BF16)
            q_unit, k_unit = units[0, i, h], units[1, i, h]
            q_part = dot(score_grad, k_unit.astype(BF16), (1, 0))
            k_part = dot(score_grad, q_unit.astype(BF16), (0, 0))
            dgrad[0, i, :, cols] = norm_back(q_part, q_unit, scales[0, i, h]).astype(BF16)
            dgrad[1, i, :, cols] = norm_back(k_part, k_unit, scales[1, i, h]).astype(BF16)

    def in_project(i):
        @pl.loop(0, D // step)
        def _(n):
            cut = pl.ds(pl.multiple_of(n * step, step), step)
            total = dot(dgrad[0, i], wq[0, cut, :], (1, 1))
            total += dot(dgrad[1, i], wq[1, cut, :], (1, 1))
            total += dot(dgrad[2, i], wq[2, cut, :], (1, 1))
            p2[i, :, cut] = total.astype(BF16)

    mixed_back(ox)
    rs1.mid_far()
    rs1.mid_x()
    mixed_back(x)
    rs1.mid_near()
    rs1.mid_x2()
    backward(ox)
    rs1.late_y()
    rs1.late_x()
    in_project(ox)
    pair2 = [pair_send(p2, q2, ox)]
    backward(x)
    rs2 = Scatter(p2, rx2, rp2, rm2)
    pair_sum(p2, q2, ox, pair2[0])
    rs2.far()
    in_project(x)
    pair2.append(pair_send(p2, q2, x))
    keep_g = pltpu.make_async_copy(T(g2, x, y, ALL), grads_ref.at[0, 0], out_sem.at[1])
    keep_g.start()
    rs1.end()
    out0[...] = (-rs1.total()).astype(BF16)
    keep_0 = pltpu.make_async_copy(out0, rebuilt_ref.at[0, 0], out_sem.at[2])
    keep_0.start()
    pair_sum(p2, q2, x, pair2[1])
    rs2.near()
    rs2.mid_far()
    rs2.mid_x()
    rs2.mid_near()
    rs2.mid_x2()
    rs2.late_y()
    rs2.late_x()
    hop_gc.wait_recv()
    rs2.end()
    normed_grad = rs2.total()
    unit_rows, inv_scale = unit_norm(g1[x, pl.ds(row(y), R), :].astype(F32))
    input_part = norm_back(normed_grad * gain[...].astype(F32), unit_rows, inv_scale)
    out1[...] = (gc1[...].astype(F32) + input_part).astype(BF16)
    keep_1 = pltpu.make_async_copy(out1, grads_ref.at[0, 1], out_sem.at[3])
    keep_1.start()
    for copy in net.copies:
        copy.wait_send()
    for keep in (keep_c, keep_g, keep_0, keep_1):
        keep.wait()


def on_device(n_section, handed_state, handed_grad, top_state, loss_grad, ln_gain, w_qkv, w_out):
    D = handed_state.shape[-1]
    width = w_out.shape[1]
    big = pltpu.VMEM((2, 8 * R, D), BF16)
    half = pltpu.VMEM((2, 4 * R, D), BF16)
    rows = pltpu.VMEM((R, D), BF16)
    recv = pltpu.VMEM((4, R, D), BF16)
    tok = 8 * R
    scratch = [
        big, big, big, rows, rows, rows,
        pltpu.VMEM((3, D, width), BF16), pltpu.VMEM((width, D), BF16),
        big, half, big, half, recv, recv, recv, recv, recv, recv,
        pltpu.VMEM((3, 2, 2, tok, HD), F32), pltpu.VMEM((2, 2, 2, tok, HD), F32), pltpu.VMEM((2, 2, 2, tok, 1), F32),
        pltpu.VMEM((2, 2, tok, tok), F32), pltpu.VMEM((2, tok, width), BF16), pltpu.VMEM((2, tok, width), BF16),
        pltpu.VMEM((3, 2, tok, width), BF16), pltpu.VMEM((1, D), BF16), rows, rows,
        pltpu.SemaphoreType.DMA((N_COPIES,)), pltpu.SemaphoreType.DMA((N_COPIES,)),
        pltpu.SemaphoreType.DMA((3,)), pltpu.SemaphoreType.DMA((4,)),
    ]
    out = jax.ShapeDtypeStruct((1, 2, R, D), BF16)
    return pl.pallas_call(
        functools.partial(kernel, n_section),
        out_shape=(out, out),
        in_specs=[pl.BlockSpec(memory_space=pl.ANY)] * 7,
        out_specs=[pl.BlockSpec(memory_space=pl.ANY)] * 2,
        scratch_shapes=scratch,
        compiler_params=pltpu.CompilerParams(
            collective_id=0, has_side_effects=True, vmem_limit_bytes=60 * 2**20
        ),
        name="sublayer_back",
    )(handed_state, handed_grad, top_state, loss_grad, ln_gain, w_qkv, w_out)


def solution(mesh):
    placed = (
        P("section", None, "tensor", None),
        P("section", None, "tensor", None),
        P(None, "tensor", None),
        P(None, "tensor", None),
        P("section", None),
        P("section", None, None, "tensor"),
        P("section", "tensor", None),
    )
    return jax.shard_map(
        functools.partial(on_device, mesh.shape["section"]),
        mesh=mesh,
        in_specs=placed,
        out_specs=(P("section", None, "tensor", None), P("section", None, "tensor", None)),
        check_vma=False,
    )
```

```python
import functools

import jax
import jax.numpy as jnp
from jax import lax
from jax.experimental import pallas as pl
from jax.experimental.pallas import tpu as pltpu
from jax.sharding import PartitionSpec as P

HD = 128
MESH = pl.DeviceIdType.MESH
F32 = jnp.float32
BF16 = jnp.bfloat16
R = 32
N_SHIFT, N_SEND, N_RECV = 10, 40, 93
ORDER = (
    0, 1, 2, 3, 4, 5, 6, 7, 8, 12, 17, 16, 20, 21, 10, 11, 28, 72, 9, 14, 23, 73, 37, 24, 13, 38, 36, 40, 30, 76,
    15, 32, 80, 41, 164, 18, 64, 77, 19, 25, 29, 74, 81, 26, 44, 43, 75, 22, 39, 46, 47, 42, 31, 78, 33, 82, 45, 53,
    57, 79, 34, 88, 27, 48, 56, 60, 89, 49, 51, 59, 66, 68, 92, 50, 52, 65, 83, 117, 84, 54, 55, 85, 94, 96, 98,
    100, 35, 116, 86, 123, 122, 87, 102, 58, 61, 62, 67, 124, 125, 103, 63, 69, 70, 118, 106, 130, 131, 90, 120,
    108, 91, 110, 112, 114, 119, 126, 127, 93, 71, 121, 134, 128, 129, 95, 97, 148, 145, 99, 101, 139, 104, 132,
    133, 105, 140, 107, 136, 135, 137, 138, 109, 111, 141, 146, 147, 143, 113, 115, 150, 153, 142, 152, 149, 165,
    144, 157, 154, 151, 163, 156, 159, 155, 158, 161, 160, 162, 166,
)


def mean_last(values):
    return jnp.mean(values, axis=-1, keepdims=True)


def unit_norm(values):
    centred = values - mean_last(values)
    inv_scale = lax.rsqrt(mean_last(centred * centred) + 1e-06)
    return centred * inv_scale, inv_scale


def norm_back(grad_unit, unit_rows, inv_scale):
    first_mean = mean_last(grad_unit)
    second_mean = mean_last(grad_unit * unit_rows)
    return (grad_unit - first_mean - unit_rows * second_mean) * inv_scale


def dot(a, b, dims):
    return lax.dot_general(a, b, ((dims[:1], dims[1:]), ((), ())), preferred_element_type=F32)


class Copy:
    def __init__(self, src, dst, send_sem, recv_sem, dev):
        self.src, self.dst, self.send_sem, self.recv_sem, self.dev = src, dst, send_sem, recv_sem, dev

    def make(self):
        return pltpu.make_async_remote_copy(
            src_ref=self.src(), dst_ref=self.dst(), send_sem=self.send_sem, recv_sem=self.recv_sem,
            device_id=self.dev, device_id_type=MESH,
        )

    def start(self):
        self.make().start()

    def wait_recv(self):
        self.make().wait_recv()

    def wait_send(self):
        self.make().wait_send()


class Net:
    def __init__(self, send_sem, recv_sem):
        self.send_sem, self.recv_sem, self.sent, self.at, self.used = send_sem, recv_sem, [], {}, 0

    def recv(self, key, count=1):
        if key not in self.at:
            self.at[key], self.used = self.used, self.used + count
        return self.at[key]

    def copy(self, src, dst, dev, key):
        k = len(self.sent)
        if k >= N_SEND:
            self.sent[k - N_SEND].wait_send()
        made = Copy(src, dst, self.send_sem.at[N_SHIFT + k % N_SEND], self.recv_sem.at[self.recv(key)], dev)
        self.sent.append(made)
        return made

    def send(self, src, dst, dev, key):
        made = self.copy(src, dst, dev, key)
        made.start()
        return made


def kernel(
    n_section, state_ref, grad_ref, top_ref, loss_ref, gain_ref, wqkv_ref, wout_ref,
    first_ref, kept_c_ref, kept_g_ref, second_ref,
    g1, g2, nb, e_buf, gc0, gc1, wq, wo, p1, q1, p2, q2, rx1, rp1, rm1, rx2, rp2, rm2,
    qkv, units, scales, probs, mixed, mgrad, dgrad, gain, out0, out1, own_unit, own_scale,
    send_sem, recv_sem, pair_sem, load_sem, out_sem,
):
    D = g1.shape[-1]
    half, width = D // 2, wo.shape[0]
    a_w = -(-D // 128 * 5 // 16) * 128
    A0, B0, B1, A1 = (0, a_w), (a_w, half), (half, D - a_w), (D - a_w, D)
    BB, ALL = (a_w, D - a_w), (0, D)
    CH = (A0, B0, B1, A1)

    s = lax.axis_index("section")
    t = lax.axis_index("tensor")
    x, y, c = t // 8, (t // 2) % 4, t % 2
    ox = 1 - x
    yp, ym, y2 = (y + 1) % 4, (y + 3) % 4, (y + 2) % 4

    def dev(xx, yy, cc):
        return (s, xx * 8 + yy * 2 + cc)

    d_yp, d_ym, d_x, d_c = dev(x, yp, c), dev(x, ym, c), dev(ox, y, c), dev(x, y, 1 - c)
    d_prev = ((s + n_section - 1) % n_section, ox * 8 + y * 2 + c)
    d_next = ((s + 1) % n_section, ox * 8 + y * 2 + c)

    def row(yo, cc=None):
        return pl.multiple_of(((c if cc is None else cc) * 4 + yo) * R, R)

    def T(buf, xo, yo, cols, cc=None):
        return buf.at[xo, pl.ds(row(yo, cc), R), pl.ds(cols[0], cols[1] - cols[0])]

    def slot(buf, i, cols):
        return buf.at[i, :, pl.ds(cols[0], cols[1] - cols[0])]

    barrier = pltpu.get_barrier_semaphore()
    for d in (d_yp, d_ym, d_x, d_c, d_prev, d_next):
        pl.semaphore_signal(barrier, inc=1, device_id=d, device_id_type=MESH)
    pl.semaphore_wait(barrier, 6)

    net = Net(send_sem, recv_sem)
    copies, tasks = {}, {}
    shared = {}
    for p in "12":
        shared |= {p + m: p + "g5" for m in ("a3u", "b1m", "b2m")}
        shared |= {p + m: p + "g6" for m in ("a0d", "b1p", "b2p")}
        shared |= {p + m: p + "g7" for m in ("a0", "a3", "b1", "b2")}
    for r in ("r1", "r2"):
        shared |= {r + m: r + "gx" for m in ("x3b", "x3a3", "x3a0")}
        shared |= {r + m: r + "gp" for m in ("p3l", "p3", "p3bl", "p3b")}
        shared |= {r + m: r + "gm" for m in ("m3l", "m3", "m3bl", "m3b")}
    once = ["x0", "x1", "x2", "p0", "m0", "p2l", "m2l", "p1", "m1", "p2", "m2", "p1b", "m1b", "gx", "gp", "gm"]
    again = {"r2" + m: f"1{d}{k}" for m, (d, k) in zip(once, [(d, k) for d in "huds" for k in range(4)])}

    def recv_key(name):
        name = shared.get(name, name)
        return again.get(name, name)

    shifts = []

    def shift(name, first_src, src, k, cols, dst):
        cut = pl.ds(cols[0], cols[1] - cols[0])
        sems = send_sem.at[len(shifts)], recv_sem.at[net.recv(name)]
        last = Copy(lambda: first_src.at[k, :, cut], dst, *sems, d_prev)
        shifts.append(last)
        here = Copy(lambda: src.at[0, k, :, cut], dst, *sems, d_prev)
        copies[name] = last

        @pl.when(s == 0)
        def _():
            last.start()

        @pl.when(s != 0)
        def _():
            here.start()

    for k in range(4):
        shift(f"1h{k}", top_ref, state_ref, 0, CH[k], functools.partial(T, g1, x, y, CH[k]))
    for k in range(4):
        shift(f"2h{k}", loss_ref, grad_ref, 1, CH[k], functools.partial(T, g2, x, y, CH[k]))
    shift("e", top_ref, state_ref, 1, ALL, lambda: e_buf)
    shift("gc", loss_ref, grad_ref, 0, ALL, lambda: gc0)

    def together(key, region):
        copies[key] = Copy(region, region, net.send_sem.at[0], net.recv_sem.at[net.recv(recv_key(key))], d_c)

    loads = [
        pltpu.make_async_copy(gain_ref, gain, load_sem.at[0]),
        pltpu.make_async_copy(wout_ref.at[0], wo, load_sem.at[1]),
    ] + [
        pltpu.make_async_copy(wqkv_ref.at[0, k], wq.at[:, pl.ds(k * width, width)], load_sem.at[2 + k]) for k in range(3)
    ]
    for load in loads:
        load.start()

    places = ((ox, y), (ox, ym), (ox, yp), (ox, y2), (x, y), (x, ym), (x, yp), (x, y2))
    slots = (
        ("h0", "h1", "h2", "h3"), ("u0", "u1", "u2", "u3"), ("d0", "d1", "d2", "d3"), ("f0", "f1", "f2", "f3"),
        ("s0", "s1", "s2", "s3"), ("a0u", "g5"), ("a3d", "g6"), ("g7",),
    )
    images = {"o": ox, "x": x}
    loaded = set()

    def need(i):
        if i not in loaded:
            loaded.add(i)
            loads[i].wait()

    def task(name, arrivals, run):
        tasks[name] = (tuple(arrivals), run)

    def sending(name, arrivals, src, dst, d):
        def run():
            copies[name] = net.send(src, dst, d, recv_key(name))

        task(name, arrivals, run)

    def forwarding(name, arrivals, buf, xo, yo, cols, d):
        sending(name, arrivals, lambda: T(buf, xo, yo, cols), lambda: T(buf, xo, yo, cols), d)

    for p, buf in (("1", g1), ("2", g2)):
        for k in range(4):
            forwarding(f"{p}u{k}", (f"{p}h{k}",), buf, ox, y, CH[k], d_yp)
            forwarding(f"{p}d{k}", (f"{p}h{k}",), buf, ox, y, CH[k], d_ym)
            forwarding(f"{p}s{k}", (f"{p}h{k}",), buf, ox, y, CH[k], d_x)
        for k in (0, 1):
            forwarding(f"{p}f{k}", (f"{p}u{k}",), buf, ox, ym, CH[k], d_yp)
        for k in (2, 3):
            forwarding(f"{p}f{k}", (f"{p}d{k}",), buf, ox, yp, CH[k], d_ym)
        for k in (0, 3):
            forwarding(f"{p}a{k}u", (f"{p}s{k}",), buf, x, y, CH[k], d_yp)
            forwarding(f"{p}a{k}d", (f"{p}s{k}",), buf, x, y, CH[k], d_ym)
        for k in (1, 2):
            forwarding(f"{p}b{k}m", (f"{p}u{k}",), buf, ox, ym, CH[k], d_x)
            forwarding(f"{p}b{k}p", (f"{p}d{k}",), buf, ox, yp, CH[k], d_x)
            forwarding(f"{p}b{k}", (f"{p}f{k}",), buf, ox, y2, CH[k], d_x)
        together(f"{p}g5", functools.partial(T, buf, x, ym, (a_w, D)))
        together(f"{p}g6", functools.partial(T, buf, x, yp, (0, D - a_w)))
        together(f"{p}g7", functools.partial(T, buf, x, y2, ALL))
        forwarding(f"{p}a0", (f"{p}a0u",), buf, x, ym, CH[0], d_yp)
        forwarding(f"{p}a3", (f"{p}a3d",), buf, x, yp, CH[3], d_ym)
        for j in range(8):
            forwarding(f"{p}c{j}", [p + m for m in slots[j]], buf, *places[j], ALL, d_c)

    def normalize(place, cc):
        need(0)
        xo, yo = place

        part = pl.ds(row(yo, cc), R)
        unit_rows, _ = unit_norm(g1[xo, part, :].astype(F32))
        nb[xo, part, :] = (unit_rows * gain[...].astype(F32)).astype(BF16)

    for j in range(8):
        task(f"no{j}", ["1" + m for m in slots[j]], functools.partial(normalize, places[j], c))
        task(f"nx{j}", (f"1c{j}",), functools.partial(normalize, places[j], 1 - c))

    def project(i):
        for k in range(3):
            need(2 + k)

        @pl.loop(0, 3)
        def _(k):
            raw = dot(nb[i], wq[:, pl.ds(pl.multiple_of(k * width, width), width)], (1, 0))
            qkv[k, i, 0] = raw[:, :HD]
            qkv[k, i, 1] = raw[:, HD:]

    def head(h, base=0):
        return slice(base + h * HD, base + (h + 1) * HD)

    def forward(i):
        for h in range(2):
            q_unit, q_scale = unit_norm(qkv[0, i, h])
            k_unit, k_scale = unit_norm(qkv[1, i, h])
            units[0, i, h] = q_unit
            units[1, i, h] = k_unit
            scales[0, i, h] = q_scale
            scales[1, i, h] = k_scale
            scores = dot(q_unit.astype(BF16), k_unit.astype(BF16), (1, 1)) * HD ** (-0.5)
            exponent = jnp.exp(scores)
            prob = exponent * (1.0 / jnp.sum(exponent, axis=-1, keepdims=True))
            probs[i, h] = prob
            value = qkv[2, i, h].astype(BF16)
            mixed[i, :, head(h)] = dot(prob.astype(BF16), value, (1, 0)).astype(BF16)

    mine0 = pl.multiple_of(c * 4 * R, R)
    other0 = pl.multiple_of((1 - c) * 4 * R, R)
    step = D // 4

    pair_sent = []

    def in_steps(names, p, q, i, value):
        at = net.recv(names[0] + names[2:], 4)
        for copy in pair_sent:
            copy.wait_send()
        pair_sent.clear()

        def pair_copy(n):
            cut = pl.ds(n * step if isinstance(n, int) else pl.multiple_of(n * step, step), step)
            src = functools.partial(lambda cut: p.at[i, pl.ds(other0, 4 * R), cut], cut)
            dst = functools.partial(lambda cut: q.at[i, :, cut], cut)
            return Copy(src, dst, pair_sem.at[n], recv_sem.at[at + n], d_c)

        @pl.loop(0, 4)
        def _(n):
            cut = pl.ds(pl.multiple_of(n * step, step), step)
            p[i, :, cut] = value(cut).astype(BF16)
            pair_copy(n).start()

        for n in range(4):
            copies[f"{names}{n}"] = pair_copy(n)
            pair_sent.append(copies[f"{names}{n}"])

    def out_project(names, i):
        need(1)
        in_steps(names, p1, q1, i, lambda cut: dot(mixed[i], wo[:, cut], (1, 0)))

    def in_project(names, i):
        in_steps(names, p2, q2, i, lambda cut: dot(dgrad[i], wq[cut, :], (1, 1)))

    def pair_sum(p, q, i, n):
        @pl.loop(0, 4)
        def _(b):
            cut = pl.ds(n * step, step)
            mine = pl.ds(pl.multiple_of(mine0 + b * R, R), R)
            total = p[i, mine, cut].astype(F32) + q[i, pl.ds(pl.multiple_of(b * R, R), R), cut].astype(F32)
            p[i, mine, cut] = total.astype(BF16)

    def mixed_back(i):
        mgrad[i] = dot(g2[i], wo[...], (1, 1)).astype(BF16)

    def backward(i):
        for h in range(2):
            mg = mgrad[i, :, head(h)]
            value = qkv[2, i, h].astype(BF16)
            prob = probs[i, h]
            prob_grad = dot(mg, value, (1, 1))
            v_grad = dot(prob.astype(BF16), mg, (0, 0)).astype(BF16)
            inner = jnp.sum(prob_grad * prob, axis=-1, keepdims=True)
            score_grad = (prob * (prob_grad - inner) * HD ** (-0.5)).astype(BF16)
            q_unit, k_unit = units[0, i, h], units[1, i, h]
            q_part = dot(score_grad, k_unit.astype(BF16), (1, 0))
            k_part = dot(score_grad, q_unit.astype(BF16), (0, 0))
            dgrad[i, :, head(h)] = norm_back(q_part, q_unit, scales[0, i, h]).astype(BF16)
            dgrad[i, :, head(h, width)] = norm_back(k_part, k_unit, scales[1, i, h]).astype(BF16)
            dgrad[i, :, head(h, 2 * width)] = v_grad

    for im, i in images.items():
        places_of = range(0, 4) if im == "o" else range(4, 8)
        task(f"pj{im}", (), functools.partial(project, i))
        task(f"fw{im}", (), functools.partial(forward, i))
        arrivals = [f"2c{j}" for j in places_of] + ["2" + m for j in places_of for m in slots[j]]
        task(f"mb{im}", arrivals, functools.partial(mixed_back, i))
        task(f"bw{im}", (), functools.partial(backward, i))
        task(f"op{im}", (), functools.partial(out_project, f"q1{im}", i))
        task(f"ip{im}", (), functools.partial(in_project, f"q2{im}", i))
        for n in range(4):
            task(f"ps1{im}{n}", (f"q1{im}{n}",), functools.partial(pair_sum, p1, q1, i, n))
            task(f"ps2{im}{n}", (f"q2{im}{n}",), functools.partial(pair_sum, p2, q2, i, n))

    def subtract():
        r0 = row(y)
        p1[ox, pl.ds(r0, R), :] = (p1[ox, pl.ds(r0, R), :].astype(F32) - e_buf[...].astype(F32)).astype(BF16)

    task("es", ("e",), subtract)
    sending("hop", ("gc",), lambda: gc0, lambda: gc1, d_x)

    def add_to(p, xo, yo, recv, i, cols):
        cut = pl.ds(cols[0], cols[1] - cols[0])
        r0 = row(yo)
        mine = p[xo, pl.ds(r0, R), cut].astype(F32)
        p[xo, pl.ds(r0, R), cut] = (mine + recv[i, :, cut].astype(F32)).astype(BF16)

    def scatter(n, p, rx, rp, rm):
        def step(name, adds, sends):
            def run():
                for xo, yo, recv, i, cols, _ in adds:
                    add_to(p, xo, yo, recv, i, cols)
                for copy, xo, yo, cols, recv, i, d in sends:
                    src = functools.partial(T, p, xo, yo, cols)
                    copies[n + copy] = net.send(src, functools.partial(slot, recv, i, cols), d, recv_key(n + copy))

            task(n + name, [n + add[-1] for add in adds], run)

        step("x0", (), (("x0", ox, y2, BB, rx, 0, d_x),))
        step("x1", (), (("x1", ox, yp, BB, rx, 1, d_x),))
        step("x2", (), (("x2", ox, ym, BB, rx, 2, d_x),))
        step("x3b", (), (("x3b", ox, y, BB, rx, 3, d_x),))
        step("p0", (), (("p0", ox, y2, A0, rp, 0, d_ym),))
        step("m0", (), (("m0", ox, y2, A1, rm, 0, d_yp),))
        step("p2l", (), (("p2l", ox, ym, A1, rp, 2, d_ym),))
        step("m2l", (), (("m2l", ox, yp, A0, rm, 2, d_yp),))
        step("p1", (), (("p1", x, y2, A0, rp, 1, d_ym),))
        step("m1", (), (("m1", x, y2, A1, rm, 1, d_yp),))
        step("p3l", (), (("p3l", x, ym, A1, rp, 3, d_ym),))
        step("m3l", (), (("m3l", x, yp, A0, rm, 3, d_yp),))
        step("p2", ((ox, ym, rp, 0, A0, "p0"),), (("p2", ox, ym, A0, rp, 2, d_ym),))
        step("m2", ((ox, yp, rm, 0, A1, "m0"),), (("m2", ox, yp, A1, rm, 2, d_yp),))
        step("p3", ((x, ym, rp, 1, A0, "p1"),), (("p3", x, ym, A0, rp, 3, d_ym),))
        step("m3", ((x, yp, rm, 1, A1, "m1"),), (("m3", x, yp, A1, rm, 3, d_yp),))
        step("tx0", ((x, y2, rx, 0, BB, "x0"),), (("p1b", x, y2, B0, rp, 1, d_ym), ("m1b", x, y2, B1, rm, 1, d_yp)))
        step("tx1", ((x, yp, rx, 1, BB, "x1"),), (("m3bl", x, yp, B0, rm, 3, d_yp),))
        step("tx2", ((x, ym, rx, 2, BB, "x2"),), (("p3bl", x, ym, B1, rp, 3, d_ym),))
        step("p3b", ((x, ym, rp, 1, B0, "p1b"),), (("p3b", x, ym, B0, rp, 3, d_ym),))
        step("m3b", ((x, yp, rm, 1, B1, "m1b"),), (("m3b", x, yp, B1, rm, 3, d_yp),))
        step("x3a3", ((ox, y, rp, 2, A1, "p2l"), (ox, y, rm, 2, A1, "m2")), (("x3a3", ox, y, A1, rx, 3, d_x),))
        step("x3a0", ((ox, y, rm, 2, A0, "m2l"), (ox, y, rp, 2, A0, "p2")), (("x3a0", ox, y, A0, rx, 3, d_x),))

    ends = ("gx", "gp", "gm")
    for r, buffers in (("r1", (rx1, rp1, rm1)), ("r2", (rx2, rp2, rm2))):
        for m, recv in zip(ends, buffers):
            together(r + m, functools.partial(slot, recv, 3, ALL))
    scatter("r1", p1, rx1, rp1, rm1)
    scatter("r2", p2, rx2, rp2, rm2)

    def total(p, rx, rp, rm):
        mine = p[x, pl.ds(row(y), R), :].astype(F32) + rx[3].astype(F32)
        return mine + (rp[3].astype(F32) + rm[3].astype(F32))

    keeps = [
        pltpu.make_async_copy(T(g1, x, y, ALL), kept_c_ref, out_sem.at[0]),
        pltpu.make_async_copy(T(g2, x, y, ALL), kept_g_ref, out_sem.at[1]),
        pltpu.make_async_copy(out0, first_ref, out_sem.at[2]),
        pltpu.make_async_copy(out1, second_ref, out_sem.at[3]),
    ]

    def finish_first():
        keeps[0].start()
        keeps[1].start()
        out0[...] = (-total(p1, rx1, rp1, rm1)).astype(BF16)
        keeps[2].start()

    def prepare():
        unit_rows, inv_scale = unit_norm(g1[x, pl.ds(row(y), R), :].astype(F32))
        own_unit[...] = unit_rows
        own_scale[...] = inv_scale

    def finish_second():
        normed_grad = total(p2, rx2, rp2, rm2)
        input_part = norm_back(normed_grad * gain[...].astype(F32), own_unit[...], own_scale[...])
        out1[...] = (gc1[...].astype(F32) + input_part).astype(BF16)
        keeps[3].start()

    task("prep", (), prepare)

    task("fin1", ["r1" + m for m in ends], finish_first)
    task("fin2", ["r2" + m for m in ends] + ["hop"], finish_second)

    arrived = set()
    names = list(tasks)
    for number in ORDER:
        arrivals, run = tasks.pop(names[number])
        for copy in arrivals:
            if copy not in arrived:
                arrived.add(copy)
                copies[copy].wait_recv()
        run()
    assert not tasks and arrived == set(copies) - set(shared)
    for copy in shifts + net.sent[-N_SEND:] + pair_sent:
        copy.wait_send()
    for keep in keeps:
        keep.wait()


def on_device(n_section, handed_state, handed_grad, top_state, loss_grad, ln_gain, w_qkv, w_out):
    D = handed_state.shape[-1]
    width = w_out.shape[1]
    big = pltpu.VMEM((2, 8 * R, D), BF16)
    half = pltpu.VMEM((2, 4 * R, D), BF16)
    rows = pltpu.VMEM((R, D), BF16)
    recv = pltpu.VMEM((4, R, D), BF16)
    tok = 8 * R
    scratch = [
        big, big, big, rows, rows, rows,
        pltpu.VMEM((D, 3 * width), BF16), pltpu.VMEM((width, D), BF16),
        big, half, big, half, recv, recv, recv, recv, recv, recv,
        pltpu.VMEM((3, 2, 2, tok, HD), F32), pltpu.VMEM((2, 2, 2, tok, HD), F32), pltpu.VMEM((2, 2, 2, tok, 1), F32),
        pltpu.VMEM((2, 2, tok, tok), F32), pltpu.VMEM((2, tok, width), BF16), pltpu.VMEM((2, tok, width), BF16),
        pltpu.VMEM((2, tok, 3 * width), BF16), pltpu.VMEM((1, D), BF16), rows, rows, pltpu.VMEM((R, D), F32), pltpu.VMEM((R, 1), F32),
        pltpu.SemaphoreType.DMA((N_SHIFT + N_SEND,)), pltpu.SemaphoreType.DMA((N_RECV,)), pltpu.SemaphoreType.DMA((4,)),
        pltpu.SemaphoreType.DMA((5,)), pltpu.SemaphoreType.DMA((4,)),
    ]
    block = jax.ShapeDtypeStruct((R, D), BF16)
    out = jax.ShapeDtypeStruct((1, 2, R, D), BF16)
    anywhere = pl.BlockSpec(memory_space=pl.ANY)
    blocks = pl.pallas_call(
        functools.partial(kernel, n_section),
        out_shape=(block,) * 4,
        in_specs=[anywhere] * 7,
        out_specs=[anywhere] * 4,
        scratch_shapes=scratch,
        compiler_params=pltpu.CompilerParams(
            collective_id=0, has_side_effects=True, vmem_limit_bytes=60 * 2**20
        ),
        name="sublayer_back",
    )(handed_state, handed_grad, top_state, loss_grad, ln_gain, w_qkv, w_out)
    vmem = pl.BlockSpec(memory_space=pltpu.VMEM)
    return pl.pallas_call(
        assemble,
        out_shape=(out, out),
        in_specs=[anywhere] * 4,
        out_specs=[anywhere] * 2,
        scratch_shapes=[pltpu.VMEM((4, R, D), BF16), pltpu.SemaphoreType.DMA((4,)), pltpu.SemaphoreType.DMA((4,))],
        name="assemble",
    )(*blocks)


def assemble(first_ref, kept_c_ref, kept_g_ref, second_ref, rebuilt_ref, grads_ref, rows, in_sem, out_sem):
    ins = (first_ref, kept_c_ref, kept_g_ref, second_ref)
    outs = (rebuilt_ref.at[0, 0], rebuilt_ref.at[0, 1], grads_ref.at[0, 0], grads_ref.at[0, 1])
    loads = [pltpu.make_async_copy(src, rows.at[i], in_sem.at[i]) for i, src in enumerate(ins)]
    stores = [pltpu.make_async_copy(rows.at[i], dst, out_sem.at[i]) for i, dst in enumerate(outs)]
    for load in loads:
        load.start()
    for load, store in zip(loads, stores):
        load.wait()
        store.start()
    for store in stores:
        store.wait()


def solution(mesh):
    placed = (
        P("section", None, "tensor", None),
        P("section", None, "tensor", None),
        P(None, "tensor", None),
        P(None, "tensor", None),
        P("section", None),
        P("section", None, None, "tensor"),
        P("section", "tensor", None),
    )
    return jax.shard_map(
        functools.partial(on_device, mesh.shape["section"]),
        mesh=mesh,
        in_specs=placed,
        out_specs=(P("section", None, "tensor", None), P("section", None, "tensor", None)),
        check_vma=False,
    )
```

```python
import functools

import jax
import jax.numpy as jnp
from jax import lax
from jax.experimental import pallas as pl
from jax.experimental.pallas import tpu as pltpu
from jax.sharding import PartitionSpec as P

HD = 128
MESH = pl.DeviceIdType.MESH
F32 = jnp.float32
BF16 = jnp.bfloat16
R = 32
N_SHIFT, N_SEND, N_RECV = 10, 40, 93
ORDER = (
    0, 1, 2, 3, 4, 5, 6, 7, 8, 12, 17, 16, 20, 21, 10, 11, 28, 72, 9, 14, 23, 73, 37, 24, 13, 38, 36, 40, 30, 76,
    15, 32, 80, 41, 164, 18, 64, 77, 19, 25, 29, 74, 81, 26, 44, 43, 75, 22, 39, 46, 47, 42, 31, 78, 33, 82, 45, 53,
    57, 79, 34, 88, 27, 48, 56, 60, 89, 49, 51, 59, 66, 68, 92, 50, 52, 65, 83, 117, 84, 54, 55, 85, 94, 96, 98,
    100, 35, 116, 86, 123, 122, 87, 102, 58, 61, 62, 67, 124, 125, 103, 63, 69, 70, 118, 106, 130, 131, 90, 120,
    108, 91, 110, 112, 114, 119, 126, 127, 93, 71, 121, 134, 128, 129, 95, 97, 148, 145, 99, 101, 139, 104, 132,
    133, 105, 140, 107, 136, 135, 137, 138, 109, 111, 141, 146, 147, 143, 113, 115, 150, 153, 142, 152, 149, 165,
    144, 157, 154, 151, 163, 156, 159, 155, 158, 161, 160, 162, 166,
)


def mean_last(values):
    return jnp.mean(values, axis=-1, keepdims=True)


def unit_norm(values):
    centred = values - mean_last(values)
    inv_scale = lax.rsqrt(mean_last(centred * centred) + 1e-06)
    return centred * inv_scale, inv_scale


def norm_back(grad_unit, unit_rows, inv_scale):
    first_mean = mean_last(grad_unit)
    second_mean = mean_last(grad_unit * unit_rows)
    return (grad_unit - first_mean - unit_rows * second_mean) * inv_scale


def dot(a, b, dims):
    return lax.dot_general(a, b, ((dims[:1], dims[1:]), ((), ())), preferred_element_type=F32)


class Copy:
    def __init__(self, src, dst, send_sem, recv_sem, dev):
        self.src, self.dst, self.send_sem, self.recv_sem, self.dev = src, dst, send_sem, recv_sem, dev

    def make(self):
        return pltpu.make_async_remote_copy(
            src_ref=self.src(), dst_ref=self.dst(), send_sem=self.send_sem, recv_sem=self.recv_sem,
            device_id=self.dev, device_id_type=MESH,
        )

    def start(self):
        self.make().start()

    def wait_recv(self):
        self.make().wait_recv()

    def wait_send(self):
        self.make().wait_send()


class Net:
    def __init__(self, send_sem, recv_sem):
        self.send_sem, self.recv_sem, self.sent, self.at, self.used = send_sem, recv_sem, [], {}, 0

    def recv(self, key, count=1):
        if key not in self.at:
            self.at[key], self.used = self.used, self.used + count
        return self.at[key]

    def copy(self, src, dst, dev, key):
        k = len(self.sent)
        if k >= N_SEND:
            self.sent[k - N_SEND].wait_send()
        made = Copy(src, dst, self.send_sem.at[N_SHIFT + k % N_SEND], self.recv_sem.at[self.recv(key)], dev)
        self.sent.append(made)
        return made

    def send(self, src, dst, dev, key):
        made = self.copy(src, dst, dev, key)
        made.start()
        return made


def kernel(
    n_section, state_ref, grad_ref, top_ref, loss_ref, gain_ref, wqkv_ref, wout_ref,
    first_ref, kept_c_ref, kept_g_ref, second_ref,
    g1, g2, nb, e_buf, gc0, gc1, wq, wo, p1, q1, p2, q2, rx1, rp1, rm1, rx2, rp2, rm2,
    qkv, units, scales, probs, mixed, mgrad, dgrad, gain, own_unit, own_scale,
    send_sem, recv_sem, pair_sem, load_sem, out_sem,
):
    D = g1.shape[-1]
    half, width = D // 2, wo.shape[0]
    a_w = -(-D // 128 * 5 // 16) * 128
    A0, B0, B1, A1 = (0, a_w), (a_w, half), (half, D - a_w), (D - a_w, D)
    BB, ALL = (a_w, D - a_w), (0, D)
    CH = (A0, B0, B1, A1)

    s = lax.axis_index("section")
    t = lax.axis_index("tensor")
    x, y, c = t // 8, (t // 2) % 4, t % 2
    ox = 1 - x
    yp, ym, y2 = (y + 1) % 4, (y + 3) % 4, (y + 2) % 4

    def dev(xx, yy, cc):
        return (s, xx * 8 + yy * 2 + cc)

    d_yp, d_ym, d_x, d_c = dev(x, yp, c), dev(x, ym, c), dev(ox, y, c), dev(x, y, 1 - c)
    d_prev = ((s + n_section - 1) % n_section, ox * 8 + y * 2 + c)
    d_next = ((s + 1) % n_section, ox * 8 + y * 2 + c)

    def row(yo, cc=None):
        return pl.multiple_of(((c if cc is None else cc) * 4 + yo) * R, R)

    def T(buf, xo, yo, cols, cc=None):
        return buf.at[xo, pl.ds(row(yo, cc), R), pl.ds(cols[0], cols[1] - cols[0])]

    def slot(buf, i, cols):
        return buf.at[i, :, pl.ds(cols[0], cols[1] - cols[0])]

    barrier = pltpu.get_barrier_semaphore()
    for d in (d_yp, d_ym, d_x, d_c, d_prev, d_next):
        pl.semaphore_signal(barrier, inc=1, device_id=d, device_id_type=MESH)
    pl.semaphore_wait(barrier, 6)

    net = Net(send_sem, recv_sem)
    copies, tasks = {}, {}
    shared = {}
    for p in "12":
        shared |= {p + m: p + "g5" for m in ("a3u", "b1m", "b2m")}
        shared |= {p + m: p + "g6" for m in ("a0d", "b1p", "b2p")}
        shared |= {p + m: p + "g7" for m in ("a0", "a3", "b1", "b2")}
    for r in ("r1", "r2"):
        shared |= {r + m: r + "gx" for m in ("x3b", "x3a3", "x3a0")}
        shared |= {r + m: r + "gp" for m in ("p3l", "p3", "p3bl", "p3b")}
        shared |= {r + m: r + "gm" for m in ("m3l", "m3", "m3bl", "m3b")}
    once = ["x0", "x1", "x2", "p0", "m0", "p2l", "m2l", "p1", "m1", "p2", "m2", "p1b", "m1b", "gx", "gp", "gm"]
    again = {"r2" + m: f"1{d}{k}" for m, (d, k) in zip(once, [(d, k) for d in "huds" for k in range(4)])}

    def recv_key(name):
        name = shared.get(name, name)
        return again.get(name, name)

    shifts = []

    def shift(name, first_src, src, k, cols, dst):
        cut = pl.ds(cols[0], cols[1] - cols[0])
        sems = send_sem.at[len(shifts)], recv_sem.at[net.recv(name)]
        last = Copy(lambda: first_src.at[k, :, cut], dst, *sems, d_prev)
        shifts.append(last)
        here = Copy(lambda: src.at[0, k, :, cut], dst, *sems, d_prev)
        copies[name] = last

        @pl.when(s == 0)
        def _():
            last.start()

        @pl.when(s != 0)
        def _():
            here.start()

    for k in range(4):
        shift(f"1h{k}", top_ref, state_ref, 0, CH[k], functools.partial(T, g1, x, y, CH[k]))
    for k in range(4):
        shift(f"2h{k}", loss_ref, grad_ref, 1, CH[k], functools.partial(T, g2, x, y, CH[k]))
    shift("e", top_ref, state_ref, 1, ALL, lambda: e_buf)
    shift("gc", loss_ref, grad_ref, 0, ALL, lambda: gc0)

    def together(key, region):
        copies[key] = Copy(region, region, net.send_sem.at[0], net.recv_sem.at[net.recv(recv_key(key))], d_c)

    loads = [
        pltpu.make_async_copy(gain_ref, gain, load_sem.at[0]),
        pltpu.make_async_copy(wout_ref.at[0], wo, load_sem.at[1]),
    ] + [
        pltpu.make_async_copy(wqkv_ref.at[0, k], wq.at[:, pl.ds(k * width, width)], load_sem.at[2 + k]) for k in range(3)
    ]
    for load in loads:
        load.start()

    places = ((ox, y), (ox, ym), (ox, yp), (ox, y2), (x, y), (x, ym), (x, yp), (x, y2))
    slots = (
        ("h0", "h1", "h2", "h3"), ("u0", "u1", "u2", "u3"), ("d0", "d1", "d2", "d3"), ("f0", "f1", "f2", "f3"),
        ("s0", "s1", "s2", "s3"), ("a0u", "g5"), ("a3d", "g6"), ("g7",),
    )
    images = {"o": ox, "x": x}
    loaded = set()

    def need(i):
        if i not in loaded:
            loaded.add(i)
            loads[i].wait()

    def task(name, arrivals, run):
        tasks[name] = (tuple(arrivals), run)

    def sending(name, arrivals, src, dst, d):
        def run():
            copies[name] = net.send(src, dst, d, recv_key(name))

        task(name, arrivals, run)

    def forwarding(name, arrivals, buf, xo, yo, cols, d):
        sending(name, arrivals, lambda: T(buf, xo, yo, cols), lambda: T(buf, xo, yo, cols), d)

    for p, buf in (("1", g1), ("2", g2)):
        for k in range(4):
            forwarding(f"{p}u{k}", (f"{p}h{k}",), buf, ox, y, CH[k], d_yp)
            forwarding(f"{p}d{k}", (f"{p}h{k}",), buf, ox, y, CH[k], d_ym)
            forwarding(f"{p}s{k}", (f"{p}h{k}",), buf, ox, y, CH[k], d_x)
        for k in (0, 1):
            forwarding(f"{p}f{k}", (f"{p}u{k}",), buf, ox, ym, CH[k], d_yp)
        for k in (2, 3):
            forwarding(f"{p}f{k}", (f"{p}d{k}",), buf, ox, yp, CH[k], d_ym)
        for k in (0, 3):
            forwarding(f"{p}a{k}u", (f"{p}s{k}",), buf, x, y, CH[k], d_yp)
            forwarding(f"{p}a{k}d", (f"{p}s{k}",), buf, x, y, CH[k], d_ym)
        for k in (1, 2):
            forwarding(f"{p}b{k}m", (f"{p}u{k}",), buf, ox, ym, CH[k], d_x)
            forwarding(f"{p}b{k}p", (f"{p}d{k}",), buf, ox, yp, CH[k], d_x)
            forwarding(f"{p}b{k}", (f"{p}f{k}",), buf, ox, y2, CH[k], d_x)
        together(f"{p}g5", functools.partial(T, buf, x, ym, (a_w, D)))
        together(f"{p}g6", functools.partial(T, buf, x, yp, (0, D - a_w)))
        together(f"{p}g7", functools.partial(T, buf, x, y2, ALL))
        forwarding(f"{p}a0", (f"{p}a0u",), buf, x, ym, CH[0], d_yp)
        forwarding(f"{p}a3", (f"{p}a3d",), buf, x, yp, CH[3], d_ym)
        for j in range(8):
            forwarding(f"{p}c{j}", [p + m for m in slots[j]], buf, *places[j], ALL, d_c)

    def normalize(place, cc):
        need(0)
        xo, yo = place

        part = pl.ds(row(yo, cc), R)
        unit_rows, _ = unit_norm(g1[xo, part, :].astype(F32))
        nb[xo, part, :] = (unit_rows * gain[...].astype(F32)).astype(BF16)

    for j in range(8):
        task(f"no{j}", ["1" + m for m in slots[j]], functools.partial(normalize, places[j], c))
        task(f"nx{j}", (f"1c{j}",), functools.partial(normalize, places[j], 1 - c))

    def project(i):
        for k in range(3):
            need(2 + k)

        @pl.loop(0, 3)
        def _(k):
            raw = dot(nb[i], wq[:, pl.ds(pl.multiple_of(k * width, width), width)], (1, 0))
            qkv[k, i, 0] = raw[:, :HD]
            qkv[k, i, 1] = raw[:, HD:]

    def head(h, base=0):
        return slice(base + h * HD, base + (h + 1) * HD)

    def forward(i):
        for h in range(2):
            q_unit, q_scale = unit_norm(qkv[0, i, h])
            k_unit, k_scale = unit_norm(qkv[1, i, h])
            units[0, i, h] = q_unit
            units[1, i, h] = k_unit
            scales[0, i, h] = q_scale
            scales[1, i, h] = k_scale
            scores = dot(q_unit.astype(BF16), k_unit.astype(BF16), (1, 1)) * HD ** (-0.5)
            exponent = jnp.exp(scores)
            prob = exponent * (1.0 / jnp.sum(exponent, axis=-1, keepdims=True))
            probs[i, h] = prob
            value = qkv[2, i, h].astype(BF16)
            mixed[i, :, head(h)] = dot(prob.astype(BF16), value, (1, 0)).astype(BF16)

    mine0 = pl.multiple_of(c * 4 * R, R)
    other0 = pl.multiple_of((1 - c) * 4 * R, R)
    step = D // 4

    pair_sent = []

    def in_steps(names, p, q, i, value):
        at = net.recv(names[0] + names[2:], 4)
        for copy in pair_sent:
            copy.wait_send()
        pair_sent.clear()

        def pair_copy(n):
            cut = pl.ds(n * step if isinstance(n, int) else pl.multiple_of(n * step, step), step)
            src = functools.partial(lambda cut: p.at[i, pl.ds(other0, 4 * R), cut], cut)
            dst = functools.partial(lambda cut: q.at[i, :, cut], cut)
            return Copy(src, dst, pair_sem.at[n], recv_sem.at[at + n], d_c)

        @pl.loop(0, 4)
        def _(n):
            cut = pl.ds(pl.multiple_of(n * step, step), step)
            p[i, :, cut] = value(cut).astype(BF16)
            pair_copy(n).start()

        for n in range(4):
            copies[f"{names}{n}"] = pair_copy(n)
            pair_sent.append(copies[f"{names}{n}"])

    def out_project(names, i):
        need(1)
        in_steps(names, p1, q1, i, lambda cut: dot(mixed[i], wo[:, cut], (1, 0)))

    def in_project(names, i):
        in_steps(names, p2, q2, i, lambda cut: dot(dgrad[i], wq[cut, :], (1, 1)))

    def pair_sum(p, q, i, n):
        @pl.loop(0, 4)
        def _(b):
            cut = pl.ds(n * step, step)
            mine = pl.ds(pl.multiple_of(mine0 + b * R, R), R)
            total = p[i, mine, cut].astype(F32) + q[i, pl.ds(pl.multiple_of(b * R, R), R), cut].astype(F32)
            p[i, mine, cut] = total.astype(BF16)

    def mixed_back(i):
        mgrad[i] = dot(g2[i], wo[...], (1, 1)).astype(BF16)

    def backward(i):
        for h in range(2):
            mg = mgrad[i, :, head(h)]
            value = qkv[2, i, h].astype(BF16)
            prob = probs[i, h]
            prob_grad = dot(mg, value, (1, 1))
            v_grad = dot(prob.astype(BF16), mg, (0, 0)).astype(BF16)
            inner = jnp.sum(prob_grad * prob, axis=-1, keepdims=True)
            score_grad = (prob * (prob_grad - inner) * HD ** (-0.5)).astype(BF16)
            q_unit, k_unit = units[0, i, h], units[1, i, h]
            q_part = dot(score_grad, k_unit.astype(BF16), (1, 0))
            k_part = dot(score_grad, q_unit.astype(BF16), (0, 0))
            dgrad[i, :, head(h)] = norm_back(q_part, q_unit, scales[0, i, h]).astype(BF16)
            dgrad[i, :, head(h, width)] = norm_back(k_part, k_unit, scales[1, i, h]).astype(BF16)
            dgrad[i, :, head(h, 2 * width)] = v_grad

    for im, i in images.items():
        places_of = range(0, 4) if im == "o" else range(4, 8)
        task(f"pj{im}", (), functools.partial(project, i))
        task(f"fw{im}", (), functools.partial(forward, i))
        arrivals = [f"2c{j}" for j in places_of] + ["2" + m for j in places_of for m in slots[j]]
        task(f"mb{im}", arrivals, functools.partial(mixed_back, i))
        task(f"bw{im}", (), functools.partial(backward, i))
        task(f"op{im}", (), functools.partial(out_project, f"q1{im}", i))
        task(f"ip{im}", (), functools.partial(in_project, f"q2{im}", i))
        for n in range(4):
            task(f"ps1{im}{n}", (f"q1{im}{n}",), functools.partial(pair_sum, p1, q1, i, n))
            task(f"ps2{im}{n}", (f"q2{im}{n}",), functools.partial(pair_sum, p2, q2, i, n))

    def subtract():
        r0 = row(y)
        p1[ox, pl.ds(r0, R), :] = (p1[ox, pl.ds(r0, R), :].astype(F32) - e_buf[...].astype(F32)).astype(BF16)

    task("es", ("e",), subtract)
    sending("hop", ("gc",), lambda: gc0, lambda: gc1, d_x)

    def add_to(p, xo, yo, recv, i, cols):
        cut = pl.ds(cols[0], cols[1] - cols[0])
        r0 = row(yo)
        mine = p[xo, pl.ds(r0, R), cut].astype(F32)
        p[xo, pl.ds(r0, R), cut] = (mine + recv[i, :, cut].astype(F32)).astype(BF16)

    def scatter(n, p, rx, rp, rm):
        def step(name, adds, sends):
            def run():
                for xo, yo, recv, i, cols, _ in adds:
                    add_to(p, xo, yo, recv, i, cols)
                for copy, xo, yo, cols, recv, i, d in sends:
                    src = functools.partial(T, p, xo, yo, cols)
                    copies[n + copy] = net.send(src, functools.partial(slot, recv, i, cols), d, recv_key(n + copy))

            task(n + name, [n + add[-1] for add in adds], run)

        step("x0", (), (("x0", ox, y2, BB, rx, 0, d_x),))
        step("x1", (), (("x1", ox, yp, BB, rx, 1, d_x),))
        step("x2", (), (("x2", ox, ym, BB, rx, 2, d_x),))
        step("x3b", (), (("x3b", ox, y, BB, rx, 3, d_x),))
        step("p0", (), (("p0", ox, y2, A0, rp, 0, d_ym),))
        step("m0", (), (("m0", ox, y2, A1, rm, 0, d_yp),))
        step("p2l", (), (("p2l", ox, ym, A1, rp, 2, d_ym),))
        step("m2l", (), (("m2l", ox, yp, A0, rm, 2, d_yp),))
        step("p1", (), (("p1", x, y2, A0, rp, 1, d_ym),))
        step("m1", (), (("m1", x, y2, A1, rm, 1, d_yp),))
        step("p3l", (), (("p3l", x, ym, A1, rp, 3, d_ym),))
        step("m3l", (), (("m3l", x, yp, A0, rm, 3, d_yp),))
        step("p2", ((ox, ym, rp, 0, A0, "p0"),), (("p2", ox, ym, A0, rp, 2, d_ym),))
        step("m2", ((ox, yp, rm, 0, A1, "m0"),), (("m2", ox, yp, A1, rm, 2, d_yp),))
        step("p3", ((x, ym, rp, 1, A0, "p1"),), (("p3", x, ym, A0, rp, 3, d_ym),))
        step("m3", ((x, yp, rm, 1, A1, "m1"),), (("m3", x, yp, A1, rm, 3, d_yp),))
        step("tx0", ((x, y2, rx, 0, BB, "x0"),), (("p1b", x, y2, B0, rp, 1, d_ym), ("m1b", x, y2, B1, rm, 1, d_yp)))
        step("tx1", ((x, yp, rx, 1, BB, "x1"),), (("m3bl", x, yp, B0, rm, 3, d_yp),))
        step("tx2", ((x, ym, rx, 2, BB, "x2"),), (("p3bl", x, ym, B1, rp, 3, d_ym),))
        step("p3b", ((x, ym, rp, 1, B0, "p1b"),), (("p3b", x, ym, B0, rp, 3, d_ym),))
        step("m3b", ((x, yp, rm, 1, B1, "m1b"),), (("m3b", x, yp, B1, rm, 3, d_yp),))
        step("x3a3", ((ox, y, rp, 2, A1, "p2l"), (ox, y, rm, 2, A1, "m2")), (("x3a3", ox, y, A1, rx, 3, d_x),))
        step("x3a0", ((ox, y, rm, 2, A0, "m2l"), (ox, y, rp, 2, A0, "p2")), (("x3a0", ox, y, A0, rx, 3, d_x),))

    ends = ("gx", "gp", "gm")
    for r, buffers in (("r1", (rx1, rp1, rm1)), ("r2", (rx2, rp2, rm2))):
        for m, recv in zip(ends, buffers):
            together(r + m, functools.partial(slot, recv, 3, ALL))
    scatter("r1", p1, rx1, rp1, rm1)
    scatter("r2", p2, rx2, rp2, rm2)

    def total(p, rx, rp, rm):
        mine = p[x, pl.ds(row(y), R), :].astype(F32) + rx[3].astype(F32)
        return mine + (rp[3].astype(F32) + rm[3].astype(F32))

    keeps = [
        pltpu.make_async_copy(T(g1, x, y, ALL), kept_c_ref, out_sem.at[0]),
        pltpu.make_async_copy(T(g2, x, y, ALL), kept_g_ref, out_sem.at[1]),
    ]

    def finish_first():
        keeps[0].start()
        keeps[1].start()
        first_ref[...] = (-total(p1, rx1, rp1, rm1)).astype(BF16)

    def prepare():
        unit_rows, inv_scale = unit_norm(g1[x, pl.ds(row(y), R), :].astype(F32))
        own_unit[...] = unit_rows
        own_scale[...] = inv_scale

    def finish_second():
        normed_grad = total(p2, rx2, rp2, rm2)
        input_part = norm_back(normed_grad * gain[...].astype(F32), own_unit[...], own_scale[...])
        second_ref[...] = (gc1[...].astype(F32) + input_part).astype(BF16)

    task("prep", (), prepare)

    task("fin1", ["r1" + m for m in ends], finish_first)
    task("fin2", ["r2" + m for m in ends] + ["hop"], finish_second)

    arrived = set()
    names = list(tasks)
    for number in ORDER:
        arrivals, run = tasks.pop(names[number])
        for copy in arrivals:
            if copy not in arrived:
                arrived.add(copy)
                copies[copy].wait_recv()
        run()
    assert not tasks and arrived == set(copies) - set(shared)
    for copy in shifts + net.sent[-N_SEND:] + pair_sent:
        copy.wait_send()
    for keep in keeps:
        keep.wait()


def on_device(n_section, handed_state, handed_grad, top_state, loss_grad, ln_gain, w_qkv, w_out):
    D = handed_state.shape[-1]
    width = w_out.shape[1]
    big = pltpu.VMEM((2, 8 * R, D), BF16)
    half = pltpu.VMEM((2, 4 * R, D), BF16)
    rows = pltpu.VMEM((R, D), BF16)
    recv = pltpu.VMEM((4, R, D), BF16)
    tok = 8 * R
    scratch = [
        big, big, big, rows, rows, rows,
        pltpu.VMEM((D, 3 * width), BF16), pltpu.VMEM((width, D), BF16),
        big, half, big, half, recv, recv, recv, recv, recv, recv,
        pltpu.VMEM((3, 2, 2, tok, HD), F32), pltpu.VMEM((2, 2, 2, tok, HD), F32), pltpu.VMEM((2, 2, 2, tok, 1), F32),
        pltpu.VMEM((2, 2, tok, tok), F32), pltpu.VMEM((2, tok, width), BF16), pltpu.VMEM((2, tok, width), BF16),
        pltpu.VMEM((2, tok, 3 * width), BF16), pltpu.VMEM((1, D), BF16), pltpu.VMEM((R, D), F32), pltpu.VMEM((R, 1), F32),
        pltpu.SemaphoreType.DMA((N_SHIFT + N_SEND,)), pltpu.SemaphoreType.DMA((N_RECV,)), pltpu.SemaphoreType.DMA((4,)),
        pltpu.SemaphoreType.DMA((5,)), pltpu.SemaphoreType.DMA((2,)),
    ]
    block = jax.ShapeDtypeStruct((R, D), BF16)
    out = jax.ShapeDtypeStruct((1, 2, R, D), BF16)
    anywhere = pl.BlockSpec(memory_space=pl.ANY)
    blocks = pl.pallas_call(
        functools.partial(kernel, n_section),
        out_shape=(pltpu.VMEM((R, D), BF16),) * 4,
        in_specs=[pl.BlockSpec(memory_space=pltpu.HBM)] * 7,
        out_specs=[pl.BlockSpec(memory_space=pltpu.VMEM)] * 4,
        scratch_shapes=scratch,
        compiler_params=pltpu.CompilerParams(
            collective_id=0, has_side_effects=True, vmem_limit_bytes=56 * 2**20
        ),
        name="sublayer_back",
    )(handed_state, handed_grad, top_state, loss_grad, ln_gain, w_qkv, w_out)
    vmem = pl.BlockSpec(memory_space=pltpu.VMEM)
    return pl.pallas_call(
        assemble,
        out_shape=(out, out),
        in_specs=[pl.BlockSpec(memory_space=pltpu.VMEM)] * 4,
        out_specs=[pl.BlockSpec(memory_space=pltpu.HBM)] * 2,
        scratch_shapes=[pltpu.SemaphoreType.DMA((4,))],
        name="assemble",
    )(*[pltpu.with_memory_space_constraint(b, pltpu.VMEM) for b in blocks])


def assemble(first_ref, kept_c_ref, kept_g_ref, second_ref, rebuilt_ref, grads_ref, sem):
    ins = (first_ref, kept_c_ref, kept_g_ref, second_ref)
    outs = (rebuilt_ref.at[0, 0], rebuilt_ref.at[0, 1], grads_ref.at[0, 0], grads_ref.at[0, 1])
    stores = [pltpu.make_async_copy(src, dst, sem.at[i]) for i, (src, dst) in enumerate(zip(ins, outs))]
    for store in stores:
        store.start()
    for store in stores:
        store.wait()


def solution(mesh):
    placed = (
        P("section", None, "tensor", None),
        P("section", None, "tensor", None),
        P(None, "tensor", None),
        P(None, "tensor", None),
        P("section", None),
        P("section", None, None, "tensor"),
        P("section", "tensor", None),
    )
    return jax.shard_map(
        functools.partial(on_device, mesh.shape["section"]),
        mesh=mesh,
        in_specs=placed,
        out_specs=(P("section", None, "tensor", None), P("section", None, "tensor", None)),
        check_vma=False,
    )
```

```python
import functools

import jax
import jax.numpy as jnp
from jax import lax
from jax.experimental import pallas as pl
from jax.experimental.pallas import tpu as pltpu
from jax.sharding import PartitionSpec as P

HD = 128
MESH = pl.DeviceIdType.MESH
F32 = jnp.float32
BF16 = jnp.bfloat16
R = 32
N_SHIFT, N_SEND, N_RECV = 10, 32, 93
ORDER = (
    0, 1, 2, 3, 4, 5, 6, 7, 8, 12, 17, 16, 20, 21, 10, 11, 28, 72, 9, 14, 23, 73, 37, 24, 13, 38, 36, 40, 30, 76,
    15, 32, 80, 164, 18, 41, 64, 77, 25, 29, 74, 19, 81, 26, 22, 75, 43, 44, 39, 46, 47, 42, 31, 78, 33, 82, 45, 53,
    57, 79, 34, 88, 27, 48, 56, 60, 89, 49, 51, 59, 66, 68, 92, 50, 52, 65, 83, 84, 117, 85, 94, 55, 54, 96, 98,
    100, 116, 35, 86, 123, 122, 87, 102, 58, 61, 62, 67, 124, 103, 63, 69, 70, 118, 125, 106, 130, 131, 90, 108,
    120, 91, 110, 112, 114, 126, 127, 93, 71, 119, 134, 128, 129, 95, 121, 97, 99, 148, 101, 145, 104, 139, 105,
    132, 133, 107, 140, 136, 135, 137, 138, 109, 111, 141, 146, 147, 113, 115, 143, 150, 153, 142, 152, 149, 165,
    144, 157, 154, 151, 163, 156, 159, 155, 158, 161, 160, 162, 166,
)


def mean_last(values):
    return jnp.mean(values, axis=-1, keepdims=True)


def unit_norm(values):
    centred = values - mean_last(values)
    inv_scale = lax.rsqrt(mean_last(centred * centred) + 1e-06)
    return centred * inv_scale, inv_scale


def norm_back(grad_unit, unit_rows, inv_scale):
    first_mean = mean_last(grad_unit)
    second_mean = mean_last(grad_unit * unit_rows)
    return (grad_unit - first_mean - unit_rows * second_mean) * inv_scale


def dot(a, b, dims):
    return lax.dot_general(a, b, ((dims[:1], dims[1:]), ((), ())), preferred_element_type=F32)


class Copy:
    def __init__(self, src, dst, send_sem, recv_sem, dev):
        self.src, self.dst, self.send_sem, self.recv_sem, self.dev = src, dst, send_sem, recv_sem, dev

    def make(self):
        return pltpu.make_async_remote_copy(
            src_ref=self.src(), dst_ref=self.dst(), send_sem=self.send_sem, recv_sem=self.recv_sem,
            device_id=self.dev, device_id_type=MESH,
        )

    def start(self):
        self.make().start()

    def wait_recv(self):
        self.make().wait_recv()

    def wait_send(self):
        self.make().wait_send()


class Net:
    def __init__(self, send_sem, recv_sem):
        self.send_sem, self.recv_sem, self.sent, self.at, self.used = send_sem, recv_sem, [], {}, 0

    def recv(self, key, count=1):
        if key not in self.at:
            self.at[key], self.used = self.used, self.used + count
        return self.at[key]

    def copy(self, src, dst, dev, key):
        k = len(self.sent)
        if k >= N_SEND:
            self.sent[k - N_SEND].wait_send()
        made = Copy(src, dst, self.send_sem.at[N_SHIFT + k % N_SEND], self.recv_sem.at[self.recv(key)], dev)
        self.sent.append(made)
        return made

    def send(self, src, dst, dev, key):
        made = self.copy(src, dst, dev, key)
        made.start()
        return made


def kernel(
    n_section, state_ref, grad_ref, top_ref, loss_ref, gain_ref, wqkv_ref, wout_ref,
    first_ref, kept_c_ref, kept_g_ref, second_ref,
    g1, g2, nb, e_buf, gc0, gc1, wq, wo, p1, q1, p2, q2, rx1, rp1, rm1, rx2, rp2, rm2,
    qkv, units, scales, probs, mixed, mgrad, dgrad, gain, own_unit, own_scale,
    send_sem, recv_sem, pair_sem, load_sem, out_sem,
):
    D = g1.shape[-1]
    half, width = D // 2, wo.shape[0]
    a_w = -(-D // 128 * 5 // 16) * 128
    A0, B0, B1, A1 = (0, a_w), (a_w, half), (half, D - a_w), (D - a_w, D)
    BB, ALL = (a_w, D - a_w), (0, D)
    CH = (A0, B0, B1, A1)

    s = lax.axis_index("section")
    t = lax.axis_index("tensor")
    x, y, c = t // 8, (t // 2) % 4, t % 2
    ox = 1 - x
    yp, ym, y2 = (y + 1) % 4, (y + 3) % 4, (y + 2) % 4

    def dev(xx, yy, cc):
        return (s, xx * 8 + yy * 2 + cc)

    d_yp, d_ym, d_x, d_c = dev(x, yp, c), dev(x, ym, c), dev(ox, y, c), dev(x, y, 1 - c)
    d_prev = ((s + n_section - 1) % n_section, ox * 8 + y * 2 + c)
    d_next = ((s + 1) % n_section, ox * 8 + y * 2 + c)

    def row(yo, cc=None):
        return pl.multiple_of(((c if cc is None else cc) * 4 + yo) * R, R)

    def T(buf, xo, yo, cols, cc=None):
        return buf.at[xo, pl.ds(row(yo, cc), R), pl.ds(cols[0], cols[1] - cols[0])]

    def slot(buf, i, cols):
        return buf.at[i, :, pl.ds(cols[0], cols[1] - cols[0])]

    barrier = pltpu.get_barrier_semaphore()
    for d in (d_yp, d_ym, d_x, d_c, d_prev, d_next):
        pl.semaphore_signal(barrier, inc=1, device_id=d, device_id_type=MESH)
    pl.semaphore_wait(barrier, 6)

    net = Net(send_sem, recv_sem)
    copies, tasks = {}, {}
    shared = {}
    for p in "12":
        shared |= {p + m: p + "g5" for m in ("a3u", "b1m", "b2m")}
        shared |= {p + m: p + "g6" for m in ("a0d", "b1p", "b2p")}
        shared |= {p + m: p + "g7" for m in ("a0", "a3", "b1", "b2")}
    for r in ("r1", "r2"):
        shared |= {r + m: r + "gx" for m in ("x3b", "x3a3", "x3a0")}
        shared |= {r + m: r + "gp" for m in ("p3l", "p3", "p3bl", "p3b")}
        shared |= {r + m: r + "gm" for m in ("m3l", "m3", "m3bl", "m3b")}
    once = ["x0", "x1", "x2", "p0", "m0", "p2l", "m2l", "p1", "m1", "p2", "m2", "p1b", "m1b", "gx", "gp", "gm"]
    again = {"r2" + m: f"1{d}{k}" for m, (d, k) in zip(once, [(d, k) for d in "huds" for k in range(4)])}

    def recv_key(name):
        name = shared.get(name, name)
        return again.get(name, name)

    shifts = []

    def shift(name, first_src, src, k, cols, dst):
        cut = pl.ds(cols[0], cols[1] - cols[0])
        sems = send_sem.at[len(shifts)], recv_sem.at[net.recv(name)]
        last = Copy(lambda: first_src.at[k, :, cut], dst, *sems, d_prev)
        shifts.append(last)
        here = Copy(lambda: src.at[0, k, :, cut], dst, *sems, d_prev)
        copies[name] = last

        @pl.when(s == 0)
        def _():
            last.start()

        @pl.when(s != 0)
        def _():
            here.start()

    for k in range(4):
        shift(f"1h{k}", top_ref, state_ref, 0, CH[k], functools.partial(T, g1, x, y, CH[k]))
    for k in range(4):
        shift(f"2h{k}", loss_ref, grad_ref, 1, CH[k], functools.partial(T, g2, x, y, CH[k]))
    shift("e", top_ref, state_ref, 1, ALL, lambda: e_buf)
    shift("gc", loss_ref, grad_ref, 0, ALL, lambda: gc0)

    def together(key, region):
        copies[key] = Copy(region, region, net.send_sem.at[0], net.recv_sem.at[net.recv(recv_key(key))], d_c)

    loads = [
        pltpu.make_async_copy(gain_ref, gain, load_sem.at[0]),
        pltpu.make_async_copy(wout_ref.at[0], wo, load_sem.at[1]),
    ] + [
        pltpu.make_async_copy(wqkv_ref.at[0, k], wq.at[:, pl.ds(k * width, width)], load_sem.at[2 + k]) for k in range(3)
    ]
    for load in loads:
        load.start()

    places = ((ox, y), (ox, ym), (ox, yp), (ox, y2), (x, y), (x, ym), (x, yp), (x, y2))
    slots = (
        ("h0", "h1", "h2", "h3"), ("u0", "u1", "u2", "u3"), ("d0", "d1", "d2", "d3"), ("f0", "f1", "f2", "f3"),
        ("s0", "s1", "s2", "s3"), ("a0u", "g5"), ("a3d", "g6"), ("g7",),
    )
    images = {"o": ox, "x": x}
    loaded = set()

    def need(i):
        if i not in loaded:
            loaded.add(i)
            loads[i].wait()

    def task(name, arrivals, run):
        tasks[name] = (tuple(arrivals), run)

    def sending(name, arrivals, src, dst, d):
        def run():
            copies[name] = net.send(src, dst, d, recv_key(name))

        task(name, arrivals, run)

    def forwarding(name, arrivals, buf, xo, yo, cols, d):
        sending(name, arrivals, lambda: T(buf, xo, yo, cols), lambda: T(buf, xo, yo, cols), d)

    for p, buf in (("1", g1), ("2", g2)):
        for k in range(4):
            forwarding(f"{p}u{k}", (f"{p}h{k}",), buf, ox, y, CH[k], d_yp)
            forwarding(f"{p}d{k}", (f"{p}h{k}",), buf, ox, y, CH[k], d_ym)
            forwarding(f"{p}s{k}", (f"{p}h{k}",), buf, ox, y, CH[k], d_x)
        for k in (0, 1):
            forwarding(f"{p}f{k}", (f"{p}u{k}",), buf, ox, ym, CH[k], d_yp)
        for k in (2, 3):
            forwarding(f"{p}f{k}", (f"{p}d{k}",), buf, ox, yp, CH[k], d_ym)
        for k in (0, 3):
            forwarding(f"{p}a{k}u", (f"{p}s{k}",), buf, x, y, CH[k], d_yp)
            forwarding(f"{p}a{k}d", (f"{p}s{k}",), buf, x, y, CH[k], d_ym)
        for k in (1, 2):
            forwarding(f"{p}b{k}m", (f"{p}u{k}",), buf, ox, ym, CH[k], d_x)
            forwarding(f"{p}b{k}p", (f"{p}d{k}",), buf, ox, yp, CH[k], d_x)
            forwarding(f"{p}b{k}", (f"{p}f{k}",), buf, ox, y2, CH[k], d_x)
        together(f"{p}g5", functools.partial(T, buf, x, ym, (a_w, D)))
        together(f"{p}g6", functools.partial(T, buf, x, yp, (0, D - a_w)))
        together(f"{p}g7", functools.partial(T, buf, x, y2, ALL))
        forwarding(f"{p}a0", (f"{p}a0u",), buf, x, ym, CH[0], d_yp)
        forwarding(f"{p}a3", (f"{p}a3d",), buf, x, yp, CH[3], d_ym)
        for j in range(8):
            forwarding(f"{p}c{j}", [p + m for m in slots[j]], buf, *places[j], ALL, d_c)

    def normalize(place, cc):
        need(0)
        xo, yo = place

        part = pl.ds(row(yo, cc), R)
        unit_rows, _ = unit_norm(g1[xo, part, :].astype(F32))
        nb[xo, part, :] = (unit_rows * gain[...].astype(F32)).astype(BF16)

    for j in range(8):
        task(f"no{j}", ["1" + m for m in slots[j]], functools.partial(normalize, places[j], c))
        task(f"nx{j}", (f"1c{j}",), functools.partial(normalize, places[j], 1 - c))

    def project(i):
        for k in range(3):
            need(2 + k)

        @pl.loop(0, 3)
        def _(k):
            raw = dot(nb[i], wq[:, pl.ds(pl.multiple_of(k * width, width), width)], (1, 0))
            qkv[k, i, 0] = raw[:, :HD]
            qkv[k, i, 1] = raw[:, HD:]

    def head(h, base=0):
        return slice(base + h * HD, base + (h + 1) * HD)

    def forward(i):
        for h in range(2):
            q_unit, q_scale = unit_norm(qkv[0, i, h])
            k_unit, k_scale = unit_norm(qkv[1, i, h])
            units[0, i, h] = q_unit
            units[1, i, h] = k_unit
            scales[0, i, h] = q_scale
            scales[1, i, h] = k_scale
            scores = dot(q_unit.astype(BF16), k_unit.astype(BF16), (1, 1)) * HD ** (-0.5)
            exponent = jnp.exp(scores)
            prob = exponent * (1.0 / jnp.sum(exponent, axis=-1, keepdims=True))
            probs[i, h] = prob
            value = qkv[2, i, h].astype(BF16)
            mixed[i, :, head(h)] = dot(prob.astype(BF16), value, (1, 0)).astype(BF16)

    mine0 = pl.multiple_of(c * 4 * R, R)
    other0 = pl.multiple_of((1 - c) * 4 * R, R)
    step = D // 4

    pair_sent = []

    def in_steps(names, p, q, i, value):
        at = net.recv(names[0] + names[2:], 4)
        for copy in pair_sent:
            copy.wait_send()
        pair_sent.clear()

        def pair_copy(n):
            cut = pl.ds(n * step if isinstance(n, int) else pl.multiple_of(n * step, step), step)
            src = functools.partial(lambda cut: p.at[i, pl.ds(other0, 4 * R), cut], cut)
            dst = functools.partial(lambda cut: q.at[i, :, cut], cut)
            return Copy(src, dst, pair_sem.at[n], recv_sem.at[at + n], d_c)

        @pl.loop(0, 4)
        def _(n):
            cut = pl.ds(pl.multiple_of(n * step, step), step)
            p[i, :, cut] = value(cut).astype(BF16)
            pair_copy(n).start()

        for n in range(4):
            copies[f"{names}{n}"] = pair_copy(n)
            pair_sent.append(copies[f"{names}{n}"])

    def out_project(names, i):
        need(1)
        in_steps(names, p1, q1, i, lambda cut: dot(mixed[i], wo[:, cut], (1, 0)))

    def in_project(names, i):
        in_steps(names, p2, q2, i, lambda cut: dot(dgrad[i], wq[cut, :], (1, 1)))

    def pair_sum(p, q, i, n):
        @pl.loop(0, 4)
        def _(b):
            cut = pl.ds(n * step, step)
            mine = pl.ds(pl.multiple_of(mine0 + b * R, R), R)
            total = p[i, mine, cut].astype(F32) + q[i, pl.ds(pl.multiple_of(b * R, R), R), cut].astype(F32)
            p[i, mine, cut] = total.astype(BF16)

    def mixed_back(i):
        mgrad[i] = dot(g2[i], wo[...], (1, 1)).astype(BF16)

    def backward(i):
        for h in range(2):
            mg = mgrad[i, :, head(h)]
            value = qkv[2, i, h].astype(BF16)
            prob = probs[i, h]
            prob_grad = dot(mg, value, (1, 1))
            v_grad = dot(prob.astype(BF16), mg, (0, 0)).astype(BF16)
            inner = jnp.sum(prob_grad * prob, axis=-1, keepdims=True)
            score_grad = (prob * (prob_grad - inner) * HD ** (-0.5)).astype(BF16)
            q_unit, k_unit = units[0, i, h], units[1, i, h]
            q_part = dot(score_grad, k_unit.astype(BF16), (1, 0))
            k_part = dot(score_grad, q_unit.astype(BF16), (0, 0))
            dgrad[i, :, head(h)] = norm_back(q_part, q_unit, scales[0, i, h]).astype(BF16)
            dgrad[i, :, head(h, width)] = norm_back(k_part, k_unit, scales[1, i, h]).astype(BF16)
            dgrad[i, :, head(h, 2 * width)] = v_grad

    for im, i in images.items():
        places_of = range(0, 4) if im == "o" else range(4, 8)
        task(f"pj{im}", (), functools.partial(project, i))
        task(f"fw{im}", (), functools.partial(forward, i))
        arrivals = [f"2c{j}" for j in places_of] + ["2" + m for j in places_of for m in slots[j]]
        task(f"mb{im}", arrivals, functools.partial(mixed_back, i))
        task(f"bw{im}", (), functools.partial(backward, i))
        task(f"op{im}", (), functools.partial(out_project, f"q1{im}", i))
        task(f"ip{im}", (), functools.partial(in_project, f"q2{im}", i))
        for n in range(4):
            task(f"ps1{im}{n}", (f"q1{im}{n}",), functools.partial(pair_sum, p1, q1, i, n))
            task(f"ps2{im}{n}", (f"q2{im}{n}",), functools.partial(pair_sum, p2, q2, i, n))

    def subtract():
        r0 = row(y)
        p1[ox, pl.ds(r0, R), :] = (p1[ox, pl.ds(r0, R), :].astype(F32) - e_buf[...].astype(F32)).astype(BF16)

    task("es", ("e",), subtract)
    sending("hop", ("gc",), lambda: gc0, lambda: gc1, d_x)

    def add_to(p, xo, yo, recv, i, cols):
        cut = pl.ds(cols[0], cols[1] - cols[0])
        r0 = row(yo)
        mine = p[xo, pl.ds(r0, R), cut].astype(F32)
        p[xo, pl.ds(r0, R), cut] = (mine + recv[i, :, cut].astype(F32)).astype(BF16)

    def scatter(n, p, rx, rp, rm):
        def step(name, adds, sends):
            def run():
                for xo, yo, recv, i, cols, _ in adds:
                    add_to(p, xo, yo, recv, i, cols)
                for copy, xo, yo, cols, recv, i, d in sends:
                    src = functools.partial(T, p, xo, yo, cols)
                    copies[n + copy] = net.send(src, functools.partial(slot, recv, i, cols), d, recv_key(n + copy))

            task(n + name, [n + add[-1] for add in adds], run)

        step("x0", (), (("x0", ox, y2, BB, rx, 0, d_x),))
        step("x1", (), (("x1", ox, yp, BB, rx, 1, d_x),))
        step("x2", (), (("x2", ox, ym, BB, rx, 2, d_x),))
        step("x3b", (), (("x3b", ox, y, BB, rx, 3, d_x),))
        step("p0", (), (("p0", ox, y2, A0, rp, 0, d_ym),))
        step("m0", (), (("m0", ox, y2, A1, rm, 0, d_yp),))
        step("p2l", (), (("p2l", ox, ym, A1, rp, 2, d_ym),))
        step("m2l", (), (("m2l", ox, yp, A0, rm, 2, d_yp),))
        step("p1", (), (("p1", x, y2, A0, rp, 1, d_ym),))
        step("m1", (), (("m1", x, y2, A1, rm, 1, d_yp),))
        step("p3l", (), (("p3l", x, ym, A1, rp, 3, d_ym),))
        step("m3l", (), (("m3l", x, yp, A0, rm, 3, d_yp),))
        step("p2", ((ox, ym, rp, 0, A0, "p0"),), (("p2", ox, ym, A0, rp, 2, d_ym),))
        step("m2", ((ox, yp, rm, 0, A1, "m0"),), (("m2", ox, yp, A1, rm, 2, d_yp),))
        step("p3", ((x, ym, rp, 1, A0, "p1"),), (("p3", x, ym, A0, rp, 3, d_ym),))
        step("m3", ((x, yp, rm, 1, A1, "m1"),), (("m3", x, yp, A1, rm, 3, d_yp),))
        step("tx0", ((x, y2, rx, 0, BB, "x0"),), (("p1b", x, y2, B0, rp, 1, d_ym), ("m1b", x, y2, B1, rm, 1, d_yp)))
        step("tx1", ((x, yp, rx, 1, BB, "x1"),), (("m3bl", x, yp, B0, rm, 3, d_yp),))
        step("tx2", ((x, ym, rx, 2, BB, "x2"),), (("p3bl", x, ym, B1, rp, 3, d_ym),))
        step("p3b", ((x, ym, rp, 1, B0, "p1b"),), (("p3b", x, ym, B0, rp, 3, d_ym),))
        step("m3b", ((x, yp, rm, 1, B1, "m1b"),), (("m3b", x, yp, B1, rm, 3, d_yp),))
        step("x3a3", ((ox, y, rp, 2, A1, "p2l"), (ox, y, rm, 2, A1, "m2")), (("x3a3", ox, y, A1, rx, 3, d_x),))
        step("x3a0", ((ox, y, rm, 2, A0, "m2l"), (ox, y, rp, 2, A0, "p2")), (("x3a0", ox, y, A0, rx, 3, d_x),))

    ends = ("gx", "gp", "gm")
    for r, buffers in (("r1", (rx1, rp1, rm1)), ("r2", (rx2, rp2, rm2))):
        for m, recv in zip(ends, buffers):
            together(r + m, functools.partial(slot, recv, 3, ALL))
    scatter("r1", p1, rx1, rp1, rm1)
    scatter("r2", p2, rx2, rp2, rm2)

    def total(p, rx, rp, rm):
        mine = p[x, pl.ds(row(y), R), :].astype(F32) + rx[3].astype(F32)
        return mine + (rp[3].astype(F32) + rm[3].astype(F32))

    keeps = [
        pltpu.make_async_copy(T(g1, x, y, ALL), kept_c_ref, out_sem.at[0]),
        pltpu.make_async_copy(T(g2, x, y, ALL), kept_g_ref, out_sem.at[1]),
    ]

    def finish_first():
        keeps[0].start()
        keeps[1].start()
        first_ref[...] = (-total(p1, rx1, rp1, rm1)).astype(BF16)

    def prepare():
        unit_rows, inv_scale = unit_norm(g1[x, pl.ds(row(y), R), :].astype(F32))
        own_unit[...] = unit_rows
        own_scale[...] = inv_scale

    def finish_second():
        normed_grad = total(p2, rx2, rp2, rm2)
        input_part = norm_back(normed_grad * gain[...].astype(F32), own_unit[...], own_scale[...])
        second_ref[...] = (gc1[...].astype(F32) + input_part).astype(BF16)

    task("prep", (), prepare)

    task("fin1", ["r1" + m for m in ends], finish_first)
    task("fin2", ["r2" + m for m in ends] + ["hop"], finish_second)

    arrived = set()
    names = list(tasks)
    for number in ORDER:
        arrivals, run = tasks.pop(names[number])
        for copy in arrivals:
            if copy not in arrived:
                arrived.add(copy)
                copies[copy].wait_recv()
        run()
    assert not tasks and arrived == set(copies) - set(shared)
    for copy in shifts + net.sent[-N_SEND:] + pair_sent:
        copy.wait_send()
    for keep in keeps:
        keep.wait()


def on_device(n_section, handed_state, handed_grad, top_state, loss_grad, ln_gain, w_qkv, w_out):
    D = handed_state.shape[-1]
    width = w_out.shape[1]
    big = pltpu.VMEM((2, 8 * R, D), BF16)
    half = pltpu.VMEM((2, 4 * R, D), BF16)
    rows = pltpu.VMEM((R, D), BF16)
    recv = pltpu.VMEM((4, R, D), BF16)
    tok = 8 * R
    scratch = [
        big, big, big, rows, rows, rows,
        pltpu.VMEM((D, 3 * width), BF16), pltpu.VMEM((width, D), BF16),
        big, half, big, half, recv, recv, recv, recv, recv, recv,
        pltpu.VMEM((3, 2, 2, tok, HD), F32), pltpu.VMEM((2, 2, 2, tok, HD), F32), pltpu.VMEM((2, 2, 2, tok, 1), F32),
        pltpu.VMEM((2, 2, tok, tok), F32), pltpu.VMEM((2, tok, width), BF16), pltpu.VMEM((2, tok, width), BF16),
        pltpu.VMEM((2, tok, 3 * width), BF16), pltpu.VMEM((1, D), BF16), pltpu.VMEM((R, D), F32), pltpu.VMEM((R, 1), F32),
        pltpu.SemaphoreType.DMA((N_SHIFT + N_SEND,)), pltpu.SemaphoreType.DMA((N_RECV,)), pltpu.SemaphoreType.DMA((4,)),
        pltpu.SemaphoreType.DMA((5,)), pltpu.SemaphoreType.DMA((2,)),
    ]
    block = jax.ShapeDtypeStruct((R, D), BF16)
    out = jax.ShapeDtypeStruct((1, 2, R, D), BF16)
    anywhere = pl.BlockSpec(memory_space=pl.ANY)
    blocks = pl.pallas_call(
        functools.partial(kernel, n_section),
        out_shape=(pltpu.VMEM((R, D), BF16),) * 4,
        in_specs=[pl.BlockSpec(memory_space=pltpu.HBM)] * 7,
        out_specs=[pl.BlockSpec(memory_space=pltpu.VMEM)] * 4,
        scratch_shapes=scratch,
        compiler_params=pltpu.CompilerParams(
            collective_id=0, has_side_effects=True, vmem_limit_bytes=56 * 2**20
        ),
        name="sublayer_back",
    )(handed_state, handed_grad, top_state, loss_grad, ln_gain, w_qkv, w_out)
    vmem = pl.BlockSpec(memory_space=pltpu.VMEM)
    return pl.pallas_call(
        assemble,
        out_shape=(out, out),
        in_specs=[pl.BlockSpec(memory_space=pltpu.VMEM)] * 4,
        out_specs=[pl.BlockSpec(memory_space=pltpu.HBM)] * 2,
        scratch_shapes=[pltpu.SemaphoreType.DMA((4,))],
        name="assemble",
    )(*[pltpu.with_memory_space_constraint(b, pltpu.VMEM) for b in blocks])


def assemble(first_ref, kept_c_ref, kept_g_ref, second_ref, rebuilt_ref, grads_ref, sem):
    ins = (first_ref, kept_c_ref, kept_g_ref, second_ref)
    outs = (rebuilt_ref.at[0, 0], rebuilt_ref.at[0, 1], grads_ref.at[0, 0], grads_ref.at[0, 1])
    stores = [pltpu.make_async_copy(src, dst, sem.at[i]) for i, (src, dst) in enumerate(zip(ins, outs))]
    for store in stores:
        store.start()
    for store in stores:
        store.wait()


def solution(mesh):
    placed = (
        P("section", None, "tensor", None),
        P("section", None, "tensor", None),
        P(None, "tensor", None),
        P(None, "tensor", None),
        P("section", None),
        P("section", None, None, "tensor"),
        P("section", "tensor", None),
    )
    return jax.shard_map(
        functools.partial(on_device, mesh.shape["section"]),
        mesh=mesh,
        in_specs=placed,
        out_specs=(P("section", None, "tensor", None), P("section", None, "tensor", None)),
        check_vma=False,
    )
```
